32 devices in a mesh: gx: 4 (over x, core), gy: 8 (over z, y).
Axes of the slice: x: 2, y: 2, z: 4, core: 2. Of those that a mesh axis runs over, the one named last changes fastest.
Arguments:
- incident: float32 [4, 8, 64, 16, 128], P('gx', 'gy'), may hold values from -8 to 8
- positions: float32 [4, 8, 3, 64], P('gx', 'gy'), as said below
- nbr_part: int32 [4, 8, 64, 60], P('gx', 'gy'), may hold values from 0 to 8, as said below
- nbr_slot: int32 [4, 8, 64, 60], P('gx', 'gy'), may hold values from 0 to 63, as said below
- nbr_count: int32 [4, 8, 64], P('gx', 'gy'), may hold values from 1 to 60, as said below
- cluster_id: int32 [4, 8, 64], P('gx', 'gy'), may hold values from 0 to 31, as said below
- mie: float32 [2, 64], replicated, may hold values from -0.45 to 0.45
- to_waves: bfloat16 [2, 64, 128], replicated, may hold values from -0.5 to 0.5
- from_waves: bfloat16 [2, 128, 64], replicated, may hold values from -0.375 to 0.375
- to_cluster: float32 [2, 64, 512], replicated, may hold values from -0.5 to 0.5
- cluster_waves: float32 [2, 512, 961], replicated, may hold values from -0.1875 to 0.1875
- centers: float32 [32, 3], replicated, as said below
Outputs:
- solution: float32 [4, 8, 64, 16, 128], P('gx', 'gy')
- expansions: float32 [32, 16, 1922], P(('gx', 'gy'))
The draws below stay inside these ranges and needn't reach their ends.
Inputs may be any that keep to these rules, and one draw needn't show every extreme that they name: `positions`: bead (i, j, b) lies in the box 2 i <= x < 2 i + 2, 2 j <= y < 2 j + 2, 0 <= z < 2. `nbr_part`: every entry names a device block that exists on the grid. `nbr_slot`: a slot never names the bead itself. Slots from nbr_count on are padding with arbitrary entries; in every draw some bead has exactly 60 valid slots. `cluster_id`: cluster a * 8 + c is a spatial box; a bead of device (i, j) belongs to cluster min(i + k, 4 - 1) * 8 + min(j + l, 8 - 1) for some k, l in the finite set (0, 1). `centers`: the centre of cluster a * 8 + c lies near the middle of its box.
All inputs are finite; a program needn't handle non-finite values.
Results may differ from the reference program's by a relative error of at most 0.0023.
Values may be sent and summed in bfloat16 or wider, within the bound.
A program may use at most 128 MiB of HBM per device.

```python
import math
import jax
import jax.numpy as jnp
from jax import lax

BEADS = 64
NEIGHBOURS = 60
FIELDS = 16
COEF = 64
WAVE_LAT = 8
WAVE_LON = 16
CL_COEF = 961
CLUSTER_LAT = 16
CLUSTER_LON = 32
WAVES = 128
CLUSTER_WAVES = 512
CLUSTERS = 32
N_GX = 4
N_GY = 8


CELL_SIZE = 2.0


def neighbour_tables(key):
    shape = (N_GX, N_GY, BEADS, NEIGHBOURS)
    base_key = jax.random.fold_in(key, 11)
    key_step_x, key_step_y, key_slots = jax.random.split(base_key, 3)
    place_x = jnp.arange(N_GX, dtype=jnp.int32).reshape(N_GX, 1, 1, 1)
    place_y = jnp.arange(N_GY, dtype=jnp.int32).reshape(1, N_GY, 1, 1)
    lower_x = jnp.where(place_x > 0, -1, 0)
    upper_x = jnp.where(place_x < N_GX - 1, 1, 0)
    lower_y = jnp.where(place_y > 0, -1, 0)
    upper_y = jnp.where(place_y < N_GY - 1, 1, 0)
    step_x = lower_x + jax.random.randint(key_step_x, shape, 0, 1 << 20) % (upper_x - lower_x + 1)
    step_y = lower_y + jax.random.randint(key_step_y, shape, 0, 1 << 20) % (upper_y - lower_y + 1)
    slots = jax.random.randint(key_slots, shape, 0, BEADS)
    bead_index = jnp.arange(BEADS, dtype=jnp.int32).reshape(1, 1, BEADS, 1)
    itself = (step_x == 0) & (step_y == 0) & (slots == bead_index)
    slots = jnp.where(itself, (slots + 1) % BEADS, slots)
    block_code = (step_x + 1) * 3 + (step_y + 1)
    return (block_code.astype(jnp.int32), slots.astype(jnp.int32))


def draw_nbr_part(key, part):
    block_code, slots = neighbour_tables(key)
    return block_code


def draw_nbr_slot(key, part):
    block_code, slots = neighbour_tables(key)
    return slots


def draw_nbr_count(key, part):
    device_count = N_GX * N_GY
    base_key = jax.random.fold_in(key, 23)
    key_caps, key_chosen, key_raw, key_top = jax.random.split(base_key, 4)
    caps = jax.random.randint(key_caps, (device_count,), NEIGHBOURS // 4, NEIGHBOURS + 1)
    chosen = jax.random.randint(key_chosen, (), 0, device_count)
    caps = jnp.where(jnp.arange(device_count, dtype=jnp.int32) == chosen, NEIGHBOURS, caps)
    raw_values = jax.random.randint(key_raw, (device_count, BEADS), 0, 1 << 20)
    counts = 1 + raw_values % caps[:, None]
    top_bead = jax.random.randint(key_top, (device_count,), 0, BEADS)
    counts = jnp.where(jnp.arange(BEADS, dtype=jnp.int32)[None, :] == top_bead[:, None], caps[:, None], counts)
    return counts.reshape(N_GX, N_GY, BEADS).astype(jnp.int32)


def half_cells(key):
    return jax.random.randint(jax.random.fold_in(key, 31), (N_GX, N_GY, 2, BEADS), 0, 2).astype(jnp.int32)


def draw_cluster_id(key, part):
    halves = half_cells(key)
    place_x = jnp.arange(N_GX, dtype=jnp.int32).reshape(N_GX, 1, 1)
    place_y = jnp.arange(N_GY, dtype=jnp.int32).reshape(1, N_GY, 1)
    box_x = jnp.minimum((2 * place_x + halves[:, :, 0] + 1) // 2, N_GX - 1)
    box_y = jnp.minimum((2 * place_y + halves[:, :, 1] + 1) // 2, N_GY - 1)
    return (box_x * N_GY + box_y).astype(jnp.int32)


def draw_positions(key, part):
    shape = (N_GX, N_GY, 3, BEADS)
    spread = jax.random.uniform(jax.random.fold_in(key, 5), shape, jnp.float32, 0.0, 1.0)
    halves = half_cells(key).astype(jnp.float32)
    column_x = jnp.arange(N_GX, dtype=jnp.float32).reshape(N_GX, 1, 1)
    column_y = jnp.arange(N_GY, dtype=jnp.float32).reshape(1, N_GY, 1)
    pos_x = CELL_SIZE * column_x + halves[:, :, 0] + spread[:, :, 0]
    pos_y = CELL_SIZE * column_y + halves[:, :, 1] + spread[:, :, 1]
    pos_z = CELL_SIZE * spread[:, :, 2]
    return jnp.stack([pos_x, pos_y, pos_z], axis=2)


def box_middle(index_count):
    index = jnp.arange(index_count, dtype=jnp.float32)
    lower = jnp.maximum(2.0 * index - 1.0, 0.0)
    upper = jnp.where(index == index_count - 1, 2.0 * index_count, 2.0 * index + 1.0)
    return 0.5 * (lower + upper)


def draw_centers(key, part):
    jitter = jax.random.uniform(jax.random.fold_in(key, 41), (N_GX, N_GY, 3), jnp.float32, -0.25, 0.25)
    middle_x = box_middle(N_GX).reshape(N_GX, 1) * jnp.ones((1, N_GY), jnp.float32)
    middle_y = box_middle(N_GY).reshape(1, N_GY) * jnp.ones((N_GX, 1), jnp.float32)
    middle_z = jnp.ones((N_GX, N_GY), jnp.float32)
    whole = jnp.stack([middle_x, middle_y, middle_z], axis=2) + jitter
    return whole.reshape(N_GX * N_GY, 3)


def levels(key, shape, shards, low, high):
    loudness, own = 1.0, jax.random.fold_in(key, 6)
    for position, blocks in shards:
        steps = jnp.exp(jax.random.uniform(jax.random.fold_in(own, position), (blocks,), jnp.float32, low / len(shards), high / len(shards)))
        loudness = loudness * jnp.repeat(steps, shape[position] // blocks).reshape([-1 if axis == position else 1 for axis in range(len(shape))])
    return loudness


def bell_draw(own_key, dims, scale, most, cuts=(), kind=jnp.bfloat16):
    values = jax.random.normal(own_key, dims, jnp.float32) * scale
    if len(cuts) > 0:
        values = levels(own_key, dims, cuts, -0.22, 0.18) * values
    return jnp.clip(values, min=-most, max=most).astype(kind)


def setup_inputs(seed: int = 0) -> dict:
    key_of = jax.random.split(jax.random.key(seed), 13)
    return {
        "incident": bell_draw(key_of[0], (N_GX, N_GY, BEADS, FIELDS, 2 * COEF), 2.0, 8.0, ((0, 4), (1, 8)), jnp.float32),
        "positions": draw_positions(jax.random.fold_in(key_of[12], 71), 0),
        "nbr_part": draw_nbr_part(jax.random.fold_in(key_of[12], 71), 0),
        "nbr_slot": draw_nbr_slot(jax.random.fold_in(key_of[12], 71), 0),
        "nbr_count": draw_nbr_count(jax.random.fold_in(key_of[12], 71), 0),
        "cluster_id": draw_cluster_id(jax.random.fold_in(key_of[12], 71), 0),
        "mie": jnp.clip(jax.random.uniform(key_of[6], (2, COEF), jnp.float32, -0.45, 0.45), -0.45, 0.45),
        "to_waves": bell_draw(key_of[7], (2, COEF, WAVES), (2 * COEF) ** -0.5, 0.5),
        "from_waves": bell_draw(key_of[8], (2, WAVES, COEF), (2 * WAVES) ** -0.5, 0.375),
        "to_cluster": bell_draw(key_of[9], (2, COEF, CLUSTER_WAVES), (2 * COEF) ** -0.5, 0.5, (), jnp.float32),
        "cluster_waves": bell_draw(key_of[10], (2, CLUSTER_WAVES, CL_COEF), (2 * CLUSTER_WAVES) ** -0.5, 0.1875, (), jnp.float32),
        "centers": draw_centers(jax.random.fold_in(key_of[12], 71), 0),
    }


WAVENUMBER = 3.0
NORM_EPSILON = 1e-06

def sphere_grid(cycle_count, cycle_size):
    polar = (jnp.arange(cycle_count, dtype=jnp.float32) + 0.5) * (math.pi / cycle_count)
    cycle_index = jnp.arange(cycle_size, dtype=jnp.float32)
    stagger = 0.5 * (jnp.arange(cycle_count, dtype=jnp.int32) % 2).astype(jnp.float32)
    azimuth = (cycle_index[None, :] + stagger[:, None]) * (2.0 * math.pi / cycle_size)
    height = jnp.cos(polar)[:, None] * jnp.ones_like(azimuth)
    radius = jnp.sin(polar)[:, None]
    return jnp.stack([(radius * jnp.cos(azimuth)).reshape(-1), (radius * jnp.sin(azimuth)).reshape(-1), height.reshape(-1)])

def block_matrix(pair):
    real_part = pair[0]
    imag_part = pair[1]
    top_half = jnp.concatenate([real_part, imag_part], axis=1)
    lower_half = jnp.concatenate([-imag_part, real_part], axis=1)
    return jnp.concatenate([top_half, lower_half], axis=0)

def times_phase(values, cos_part, sin_part):
    half_width = values.shape[-1] // 2
    real_part = values[..., :half_width]
    imag_part = values[..., half_width:]
    return jnp.concatenate([real_part * cos_part - imag_part * sin_part, real_part * sin_part + imag_part * cos_part], axis=-1)

def slot_phase(offsets, is_live, directions):
    distance = jnp.sqrt(offsets[0] * offsets[0] + offsets[1] * offsets[1] + offsets[2] * offsets[2])
    scale = jnp.where(is_live, 1.0 / (1.0 + distance), 0.0)
    along_dir = offsets[0][..., None] * directions[0] + offsets[1][..., None] * directions[1] + offsets[2][..., None] * directions[2]
    phase_angle = WAVENUMBER * along_dir
    return (scale[..., None] * jnp.cos(phase_angle), scale[..., None] * jnp.sin(phase_angle))

def products(first, second):
    return lax.optimization_barrier(jnp.sum(first * second, axis=(0, 2)))

def reference(incident, positions, nbr_part, nbr_slot, nbr_count, cluster_id, mie, to_waves, from_waves, to_cluster, cluster_waves, centers):
    beads_all = N_GX * N_GY * BEADS
    forward_matrix = block_matrix(to_waves)
    back_matrix = block_matrix(from_waves)
    directions = sphere_grid(WAVE_LAT, WAVE_LON)
    flat_pos = jnp.transpose(positions, (2, 0, 1, 3)).reshape(3, beads_all)
    row_x = jnp.arange(N_GX, dtype=jnp.int32).reshape(N_GX, 1, 1, 1)
    row_y = jnp.arange(N_GY, dtype=jnp.int32).reshape(1, N_GY, 1, 1)
    owner = (row_x + nbr_part // 3 - 1) * N_GY + (row_y + nbr_part % 3 - 1)
    global_index = (owner * BEADS + nbr_slot).reshape(beads_all, NEIGHBOURS).astype(jnp.int32)
    counts = nbr_count.reshape(beads_all)

    def apply_operator(vector):
        vector_low = vector.astype(jnp.bfloat16)
        samples = jnp.dot(vector_low.reshape(-1, 2 * COEF), forward_matrix, preferred_element_type=jnp.float32)
        samples = samples.astype(jnp.bfloat16).reshape(beads_all, FIELDS, 2 * WAVES)

        def one_slot(running, slot):
            slot_index = global_index[:, slot]
            offsets = flat_pos - flat_pos[:, slot_index]
            cos_part, sin_part = slot_phase(offsets, slot < counts, directions)
            picked = samples[slot_index].astype(jnp.float32)
            return (running + times_phase(picked, cos_part[:, None, :], sin_part[:, None, :]), None)
        start_sum = jnp.zeros((beads_all, FIELDS, 2 * WAVES), jnp.float32)
        incoming, _ = lax.scan(one_slot, start_sum, jnp.arange(NEIGHBOURS, dtype=jnp.int32))
        incoming = incoming.astype(jnp.bfloat16)
        back_vals = jnp.dot(incoming.reshape(-1, 2 * WAVES), back_matrix, preferred_element_type=jnp.float32)
        back_vals = back_vals.reshape(beads_all, FIELDS, 2 * COEF)
        return vector - times_phase(back_vals, mie[0], mie[1])
    source = times_phase(incident.reshape(beads_all, FIELDS, 2 * COEF), mie[0], mie[1])
    beta = jnp.sqrt(products(source, source) + NORM_EPSILON)
    basis_one = source / beta[None, :, None]
    image_one = apply_operator(basis_one)
    proj_one = products(basis_one, image_one)
    rest_one = image_one - proj_one[None, :, None] * basis_one
    norm_one = jnp.sqrt(products(rest_one, rest_one) + NORM_EPSILON)
    basis_two = rest_one / norm_one[None, :, None]
    image_two = apply_operator(basis_two)
    proj_cross = products(basis_one, image_two)
    proj_two = products(basis_two, image_two)
    rest_two = image_two - proj_cross[None, :, None] * basis_one - proj_two[None, :, None] * basis_two
    rest_square = products(rest_two, rest_two) + NORM_EPSILON
    gram_first = proj_one * proj_one + norm_one * norm_one
    gram_cross = proj_one * proj_cross + norm_one * proj_two
    gram_second = proj_cross * proj_cross + proj_two * proj_two + rest_square
    minor_term = proj_one * proj_two - norm_one * proj_cross
    gram_det = minor_term * minor_term + rest_square * gram_first
    weight_one = beta * (gram_second * proj_one - gram_cross * proj_cross) / gram_det
    weight_two = beta * (gram_first * proj_cross - gram_cross * proj_one) / gram_det
    solution = weight_one[None, :, None] * basis_one + weight_two[None, :, None] * basis_two
    cluster_dirs = sphere_grid(CLUSTER_LAT, CLUSTER_LON)
    cluster_forward = block_matrix(to_cluster)
    cluster_back = block_matrix(cluster_waves)
    device_count = N_GX * N_GY
    blocks_sol = solution.reshape(device_count, BEADS, FIELDS, 2 * COEF)
    blocks_pos = positions.reshape(device_count, 3, BEADS)
    blocks_id = cluster_id.reshape(device_count, BEADS)

    def add_block(totals, block_items):
        solution_block, bead_pos, cluster_ids = block_items
        samples = jnp.dot(solution_block.reshape(-1, 2 * COEF), cluster_forward, precision=lax.Precision.HIGHEST)
        samples = samples.reshape(BEADS, FIELDS, 2 * CLUSTER_WAVES)
        offsets = bead_pos - jnp.transpose(centers[cluster_ids])
        along_dir = offsets[0][:, None] * cluster_dirs[0] + offsets[1][:, None] * cluster_dirs[1] + offsets[2][:, None] * cluster_dirs[2]
        phase_angle = WAVENUMBER * along_dir
        shifted = times_phase(samples, jnp.cos(phase_angle)[:, None, :], jnp.sin(phase_angle)[:, None, :])
        return (totals + jax.ops.segment_sum(shifted.reshape(BEADS, -1), cluster_ids, num_segments=CLUSTERS), None)
    start_totals = jnp.zeros((CLUSTERS, FIELDS * 2 * CLUSTER_WAVES), jnp.float32)
    cluster_sums, _ = lax.scan(add_block, start_totals, (blocks_sol, blocks_pos, blocks_id))
    expansions = jnp.dot(cluster_sums.reshape(-1, 2 * CLUSTER_WAVES), cluster_back, precision=lax.Precision.HIGHEST)
    expansions = expansions.reshape(CLUSTERS, FIELDS, 2 * CL_COEF)
    return (solution.reshape(N_GX, N_GY, BEADS, FIELDS, 2 * COEF), expansions)
```

```python
import math

import jax
import jax.numpy as jnp
from jax import lax
from jax.sharding import PartitionSpec as P

WAVE_LAT = 8
WAVE_LON = 16
CLUSTER_LAT = 16
CLUSTER_LON = 32
WAVENUMBER = 3.0
EPS = 1e-06
HI = lax.Precision.HIGHEST


def shift(block, axis, distance):
    count = lax.axis_size(axis)
    route = [(i - distance, i) for i in range(count) if 0 <= i - distance < count]
    return lax.ppermute(block, axis, route)


def extended(block):
    column = jnp.stack([shift(block, "gy", 1), block, shift(block, "gy", -1)])
    return jnp.stack([shift(column, "gx", 1), column, shift(column, "gx", -1)])


def sphere_grid(cycle_count, cycle_size):
    polar = (jnp.arange(cycle_count, dtype=jnp.float32) + 0.5) * (math.pi / cycle_count)
    cycle_index = jnp.arange(cycle_size, dtype=jnp.float32)
    stagger = 0.5 * (jnp.arange(cycle_count, dtype=jnp.int32) % 2).astype(jnp.float32)
    azimuth = (cycle_index[None, :] + stagger[:, None]) * (2.0 * math.pi / cycle_size)
    height = jnp.cos(polar)[:, None] * jnp.ones_like(azimuth)
    radius = jnp.sin(polar)[:, None]
    return jnp.stack(
        [
            (radius * jnp.cos(azimuth)).reshape(-1),
            (radius * jnp.sin(azimuth)).reshape(-1),
            height.reshape(-1),
        ]
    )


def block_matrix(pair):
    top_half = jnp.concatenate([pair[0], pair[1]], axis=1)
    lower_half = jnp.concatenate([-pair[1], pair[0]], axis=1)
    return jnp.concatenate([top_half, lower_half], axis=0)


def times_phase(values, cos_part, sin_part):
    half_width = values.shape[-1] // 2
    real_part = values[..., :half_width]
    imag_part = values[..., half_width:]
    return jnp.concatenate(
        [real_part * cos_part - imag_part * sin_part, real_part * sin_part + imag_part * cos_part],
        axis=-1,
    )


def angles(pos, dirs):
    along = pos[0][:, None] * dirs[0] + pos[1][:, None] * dirs[1] + pos[2][:, None] * dirs[2]
    return WAVENUMBER * along


def weights(gram):
    ss, st, tt, su, tu, uu = [gram[k] for k in range(6)]
    beta2 = ss + EPS
    beta = jnp.sqrt(beta2)
    h11 = (ss - st) / beta2
    c = (st + EPS) / beta2
    rest = jnp.maximum((c * c * ss - 2.0 * c * st + tt) / beta2, 0.0)
    h21 = jnp.sqrt(rest + EPS)
    r = -1.0 / (beta * h21)
    p = -c * r
    h12 = (p * ss + (r - p) * st - r * su) / beta
    h22 = p * (p * ss + (r - p) * st - r * su) + r * (p * st + (r - p) * tt - r * tu)
    a = p - h12 / beta - h22 * p
    b = r - p - h22 * r
    g = -r
    q = a * a * ss + b * b * tt + g * g * uu + 2.0 * (a * b * st + a * g * su + b * g * tu)
    q = jnp.maximum(q, 0.0) + EPS
    gram_first = h11 * h11 + h21 * h21
    gram_cross = h11 * h12 + h21 * h22
    gram_second = h12 * h12 + h22 * h22 + q
    minor = h11 * h22 - h21 * h12
    det = minor * minor + q * gram_first
    y1 = beta * (gram_second * h11 - gram_cross * h12) / det
    y2 = beta * (gram_first * h12 - gram_cross * h11) / det
    return y1 / beta + y2 * p, y2 * r


def local(
    incident,
    positions,
    nbr_part,
    nbr_slot,
    nbr_count,
    cluster_id,
    mie,
    to_waves,
    from_waves,
    to_cluster,
    cluster_waves,
    centers,
):
    bead_count = incident.shape[2]
    field_count = incident.shape[3]
    coef_width = incident.shape[4]
    wave_count = to_waves.shape[2]
    forward_matrix = block_matrix(to_waves)
    back_matrix = block_matrix(from_waves)
    source = times_phase(jnp.transpose(incident[0, 0], (1, 0, 2)), mie[0], mie[1])
    own_pos = positions[0, 0]
    all_pos = jnp.transpose(extended(own_pos), (2, 0, 1, 3)).reshape(3, 9 * bead_count)
    flat_index = nbr_part[0, 0] * bead_count + nbr_slot[0, 0]
    slots = jnp.arange(flat_index.shape[1], dtype=jnp.int32)
    flat_index = jnp.where(slots[None, :] < nbr_count[0, 0][:, None], flat_index, -1)
    rows = jnp.arange(9 * bead_count, dtype=jnp.int32)
    times = jnp.sum((flat_index[:, :, None] == rows).astype(jnp.float32), axis=1)
    diff = own_pos[:, :, None] - all_pos[:, None, :]
    dist = jnp.sqrt(diff[0] * diff[0] + diff[1] * diff[1] + diff[2] * diff[2])
    weight = times / (1.0 + dist)
    weight_hi = weight.astype(jnp.bfloat16)
    weight_lo = (weight - weight_hi.astype(jnp.float32)).astype(jnp.bfloat16)
    weight_pair = jnp.concatenate([weight_hi, weight_lo], axis=0)
    dirs = sphere_grid(WAVE_LAT, WAVE_LON)
    own_angle = angles(own_pos, dirs)
    own_cos, own_sin = jnp.cos(own_angle), jnp.sin(own_angle)
    all_angle = angles(all_pos, dirs)
    all_cos, all_sin = jnp.cos(all_angle), jnp.sin(all_angle)

    def scatter(vector):
        low = vector.astype(jnp.bfloat16)
        blocks = extended(low)
        blocks = jnp.transpose(blocks, (2, 0, 1, 3, 4)).reshape(
            field_count, 9 * bead_count, coef_width
        )
        samples = jnp.einsum(
            "fnc,cq->fnq", blocks, forward_matrix, preferred_element_type=jnp.float32
        )
        turned = times_phase(samples, all_cos, -all_sin).astype(jnp.bfloat16)
        both = jnp.einsum("bn,fnq->fbq", weight_pair, turned, preferred_element_type=jnp.float32)
        incoming = both[:, :bead_count] + both[:, bead_count:]
        incoming = times_phase(incoming, own_cos, own_sin).astype(jnp.bfloat16)
        back = jnp.einsum(
            "fbq,qc->fbc", incoming, back_matrix, preferred_element_type=jnp.float32
        )
        return times_phase(back, mie[0], mie[1])

    once = scatter(source)
    twice = scatter(once)
    pairs = (
        (source, source),
        (source, once),
        (once, once),
        (source, twice),
        (once, twice),
        (twice, twice),
    )
    gram = jnp.stack([jnp.sum(x * y, axis=(1, 2)) for x, y in pairs])
    gram = lax.psum(gram, ("gx", "gy"))
    w_source, w_once = weights(gram)
    answer = w_source[:, None, None] * source + w_once[:, None, None] * once

    cluster_dirs = sphere_grid(CLUSTER_LAT, CLUSTER_LON)
    samples = jnp.einsum("fbc,cq->fbq", answer, block_matrix(to_cluster), precision=HI)
    bead_ids = cluster_id[0, 0]
    cluster_total = centers.shape[0]
    one_hot = (bead_ids[:, None] == jnp.arange(cluster_total, dtype=jnp.int32)[None, :]).astype(
        jnp.float32
    )
    bead_centre = jnp.dot(one_hot, centers, precision=HI)
    turn = angles(own_pos - jnp.transpose(bead_centre), cluster_dirs)
    shifted = times_phase(samples, jnp.cos(turn), jnp.sin(turn))
    span_y = lax.axis_size("gy")
    code = (bead_ids // span_y - lax.axis_index("gx")) * 2 + (
        bead_ids % span_y - lax.axis_index("gy")
    )
    hot = (jnp.arange(4, dtype=jnp.int32)[:, None] == code[None, :]).astype(jnp.float32)
    part = jnp.einsum("kb,fbq->kfq", hot, shifted, precision=HI)
    part = part.reshape(2, 2, field_count, -1)
    section = part[:, 0] + shift(part[:, 1], "gy", 1)
    own = section[0] + shift(section[1], "gx", 1)
    half = own.shape[1] // 2
    halves = jnp.concatenate([own[:, :half], own[:, half:]], axis=0)
    by_real = jnp.dot(halves, cluster_waves[0], precision=HI)
    by_imag = jnp.dot(halves, cluster_waves[1], precision=HI)
    expansions = jnp.concatenate(
        [
            by_real[:field_count] - by_imag[field_count:],
            by_imag[:field_count] + by_real[field_count:],
        ],
        axis=1,
    )
    return (jnp.transpose(answer, (1, 0, 2))[None, None], expansions[None])


def solution(mesh):
    in_specs = (
        P("gx", "gy", None, None, None),
        P("gx", "gy", None, None),
        P("gx", "gy", None, None),
        P("gx", "gy", None, None),
        P("gx", "gy", None),
        P("gx", "gy", None),
        P(),
        P(),
        P(),
        P(),
        P(),
        P(),
    )
    out_specs = (P("gx", "gy", None, None, None), P(("gx", "gy"), None, None))
    return jax.shard_map(local, mesh=mesh, in_specs=in_specs, out_specs=out_specs, check_vma=False)
```

```python
import functools
import math

import jax
import jax.numpy as jnp
from jax import lax
from jax.experimental import pallas as pl
from jax.experimental.pallas import tpu as pltpu
from jax.sharding import PartitionSpec as P

WAVE_LAT = 8
WAVE_LON = 16
CLUSTER_LAT = 16
CLUSTER_LON = 32
WAVENUMBER = 3.0
EPS = 1e-06
HI = lax.Precision.HIGHEST


def shift(block, axis, distance):
    count = lax.axis_size(axis)
    route = [(i - distance, i) for i in range(count) if 0 <= i - distance < count]
    return lax.ppermute(block, axis, route)


def sphere_grid(cycle_count, cycle_size):
    polar = (jnp.arange(cycle_count, dtype=jnp.float32) + 0.5) * (math.pi / cycle_count)
    cycle_index = jnp.arange(cycle_size, dtype=jnp.float32)
    stagger = 0.5 * (jnp.arange(cycle_count, dtype=jnp.int32) % 2).astype(jnp.float32)
    azimuth = (cycle_index[None, :] + stagger[:, None]) * (2.0 * math.pi / cycle_size)
    height = jnp.cos(polar)[:, None] * jnp.ones_like(azimuth)
    radius = jnp.sin(polar)[:, None]
    return jnp.stack(
        [
            (radius * jnp.cos(azimuth)).reshape(-1),
            (radius * jnp.sin(azimuth)).reshape(-1),
            height.reshape(-1),
        ]
    )


def block_matrix(pair):
    top_half = jnp.concatenate([pair[0], pair[1]], axis=1)
    lower_half = jnp.concatenate([-pair[1], pair[0]], axis=1)
    return jnp.concatenate([top_half, lower_half], axis=0)


def times_phase(values, cos_part, sin_part):
    half_width = values.shape[-1] // 2
    real_part = values[..., :half_width]
    imag_part = values[..., half_width:]
    return jnp.concatenate(
        [real_part * cos_part - imag_part * sin_part, real_part * sin_part + imag_part * cos_part],
        axis=-1,
    )


def angles(pos, dirs):
    along = pos[0][:, None] * dirs[0] + pos[1][:, None] * dirs[1] + pos[2][:, None] * dirs[2]
    return WAVENUMBER * along


def weights(gram):
    ss, st, tt, su, tu, uu = [gram[k] for k in range(6)]
    beta2 = ss + EPS
    beta = jnp.sqrt(beta2)
    h11 = (ss - st) / beta2
    c = (st + EPS) / beta2
    rest = jnp.maximum((c * c * ss - 2.0 * c * st + tt) / beta2, 0.0)
    h21 = jnp.sqrt(rest + EPS)
    r = -1.0 / (beta * h21)
    p = -c * r
    h12 = (p * ss + (r - p) * st - r * su) / beta
    h22 = p * (p * ss + (r - p) * st - r * su) + r * (p * st + (r - p) * tt - r * tu)
    a = p - h12 / beta - h22 * p
    b = r - p - h22 * r
    g = -r
    q = a * a * ss + b * b * tt + g * g * uu + 2.0 * (a * b * st + a * g * su + b * g * tu)
    q = jnp.maximum(q, 0.0) + EPS
    gram_first = h11 * h11 + h21 * h21
    gram_cross = h11 * h12 + h21 * h22
    gram_second = h12 * h12 + h22 * h22 + q
    minor = h11 * h22 - h21 * h12
    det = minor * minor + q * gram_first
    y1 = beta * (gram_second * h11 - gram_cross * h12) / det
    y2 = beta * (gram_first * h12 - gram_cross * h11) / det
    return y1 / beta + y2 * p, y2 * r


CHUNKS = 2
SHIFTS = [(dx, dy) for dx in (-1, 0, 1) for dy in (-1, 0, 1)]


def krylov_kernel(
    nx,
    ny,
    source,
    column_pos,
    row_pos,
    times,
    dirs,
    forward_matrix,
    back_matrix,
    mie_rows,
    once,
    gram_out,
    buf_one,
    buf_two,
    geo,
    turn_cos,
    turn_sin,
    weight,
    total,
    gram_x,
    gram_y,
    geo_send,
    geo_recv,
    one_send,
    one_recv,
    two_send,
    two_recv,
    x_send,
    x_recv,
    y_send,
    y_recv,
):
    i, j = lax.axis_index("gx"), lax.axis_index("gy")
    fields, beads, width = source.shape
    wide = turn_cos.shape[2]
    step = fields // CHUNKS

    def present(dx, dy):
        return (i + dx >= 0) & (i + dx < nx) & (j + dy >= 0) & (j + dy < ny)

    def piece(buf, p, c):
        if len(buf.shape) == 3:
            return buf.at[p]
        return buf.at[pl.ds(c * step, step), p]

    def make(buf, send, recv, slot, src, dst, c, dx, dy):
        return pltpu.make_async_remote_copy(
            src_ref=piece(buf, src, c),
            dst_ref=piece(buf, dst, c),
            send_sem=send.at[slot, c],
            recv_sem=recv.at[dst, c],
            device_id=(i + dx, j + dy),
            device_id_type=pl.DeviceIdType.MESH,
        )

    own_routes = [(0, 4, 3, 0, 1), (1, 4, 5, 0, -1), (2, 4, 1, 1, 0), (3, 4, 7, -1, 0)]
    low_routes = [(4, 3, 0, 1, 0), (5, 3, 6, -1, 0)]
    high_routes = [(6, 5, 2, 1, 0), (7, 5, 8, -1, 0)]

    def guarded(route):
        ok = present(route[3], route[4])
        if route[1] == 3:
            ok = ok & (j > 0)
        if route[1] == 5:
            ok = ok & (j < ny - 1)
        return pl.when(ok)

    def start(group, routes, c):
        for route in routes:

            @guarded(route)
            def _(route=route):
                slot, src, dst, dx, dy = route
                make(*group, slot, src, dst, c, dx, dy).start()

    def finish_sends(group, count):
        for c in range(count):
            for route in own_routes + low_routes + high_routes:

                @guarded(route)
                def _(route=route, c=c):
                    slot, src, dst, dx, dy = route
                    make(*group, slot, src, dst, c, dx, dy).wait_send()

    def arrive(group, p, c):
        dx, dy = SHIFTS[p]
        via = (dx, 0) if dx != 0 else (0, dy)

        @pl.when(present(dx, dy))
        def _():
            make(*group, 0, 4, p, c, via[0], via[1]).wait_recv()

    def forward(group, c):
        arrive(group, 3, c)
        start(group, low_routes, c)
        arrive(group, 5, c)
        start(group, high_routes, c)

    geo_group = (geo, geo_send, geo_recv)
    one_group = (buf_one, one_send, one_recv)
    two_group = (buf_two, two_send, two_recv)

    barrier = pltpu.get_barrier_semaphore()
    for d in range(1, nx):
        pl.semaphore_signal(
            barrier,
            inc=1,
            device_id=(lax.rem(i + d, nx), j),
            device_id_type=pl.DeviceIdType.MESH,
        )
    for d in range(1, ny):
        pl.semaphore_signal(
            barrier,
            inc=1,
            device_id=(i, lax.rem(j + d, ny)),
            device_id_type=pl.DeviceIdType.MESH,
        )
    geo[4] = column_pos[...]

    def to_low(f, carry):
        buf_one[f, 4] = source[f].astype(jnp.bfloat16)
        return carry

    lax.fori_loop(0, fields, to_low, 0)
    for p, (dx, dy) in enumerate(SHIFTS):

        @pl.when(jnp.logical_not(present(dx, dy)))
        def _(p=p):
            geo[p] = jnp.zeros(geo.shape[1:], geo.dtype)

            def clear(f, carry):
                buf_one[f, p] = jnp.zeros((beads, width), jnp.bfloat16)
                buf_two[f, p] = jnp.zeros((beads, width), jnp.bfloat16)
                return carry

            lax.fori_loop(0, fields, clear, 0)

    pl.semaphore_wait(barrier, nx + ny - 2)

    start(geo_group, own_routes, 0)
    for c in range(CHUNKS):
        start(one_group, own_routes, c)
    forward(geo_group, 0)

    def geometry(p):
        pos = geo[p]
        along = (
            pos[:, 0:1] * dirs[0:1, :] + pos[:, 1:2] * dirs[1:2, :] + pos[:, 2:3] * dirs[2:3, :]
        )
        angle = WAVENUMBER * along
        turn_cos[p] = jnp.cos(angle)
        turn_sin[p] = jnp.sin(angle)
        ex = row_pos[0:1, :] - pos[:, 0:1]
        ey = row_pos[1:2, :] - pos[:, 1:2]
        ez = row_pos[2:3, :] - pos[:, 2:3]
        dist = jnp.sqrt(ex * ex + ey * ey + ez * ez)
        full = times[p] / (1.0 + dist)
        high = full.astype(jnp.bfloat16).astype(jnp.float32)
        lane = lax.broadcasted_iota(jnp.int32, full.shape, 1)
        weight[p] = jnp.where(lane < beads, high, full - high).astype(jnp.bfloat16)

    geometry(4)
    for p in (3, 5):
        geometry(p)
    for c in range(CHUNKS):
        forward(one_group, c)
    for p in (0, 1, 2, 6, 7, 8):
        arrive(geo_group, p, 0)
        geometry(p)

    def gathered(buf, f, first, count):
        rows = count * beads
        spot = pl.ds(first, count)
        low = buf[f, spot].reshape(rows, width)
        smp = jnp.dot(low, forward_matrix[...], preferred_element_type=jnp.float32)
        re, im = smp[:, :wide], smp[:, wide:]
        co = turn_cos[spot].reshape(rows, wide)
        si = turn_sin[spot].reshape(rows, wide)
        turned = jnp.concatenate(
            [
                (re * co + im * si).astype(jnp.bfloat16),
                (im * co - re * si).astype(jnp.bfloat16),
            ],
            axis=1,
        )
        return lax.dot_general(
            weight[spot].reshape(rows, 2 * beads),
            turned,
            (((0,), (0,)), ((), ())),
            preferred_element_type=jnp.float32,
        )

    def back_turn(acc):
        inc = acc[:beads] + acc[beads:]
        re, im = inc[:, :wide], inc[:, wide:]
        co, si = turn_cos[4], turn_sin[4]
        inc = jnp.concatenate([re * co - im * si, re * si + im * co], axis=1)
        high = inc.astype(jnp.bfloat16)
        low = (inc - high.astype(jnp.float32)).astype(jnp.bfloat16)
        back = jnp.dot(
            jnp.concatenate([high, low], axis=0),
            back_matrix[...],
            preferred_element_type=jnp.float32,
        )
        back = back[:beads] + back[beads:]
        return back * mie_rows[0:1, :] + pltpu.roll(back, width // 2, 1) * mie_rows[1:2, :]

    def middle(buf):
        def body(f, carry):
            total[f] = gathered(buf, f, 3, 3)
            return carry

        lax.fori_loop(0, fields, body, 0)

    def sides(buf, f):
        return back_turn(total[f] + gathered(buf, f, 0, 3) + gathered(buf, f, 6, 3))

    middle(buf_one)
    for c in range(CHUNKS):
        for p in (0, 1, 2, 6, 7, 8):
            arrive(one_group, p, c)

        def first(f, carry):
            value = sides(buf_one, f)
            once[f] = value
            buf_two[f, 4] = value.astype(jnp.bfloat16)
            return carry

        lax.fori_loop(c * step, (c + 1) * step, first, 0)
        start(two_group, own_routes, c)

    for c in range(CHUNKS):
        forward(two_group, c)
    middle(buf_two)

    row = lax.broadcasted_iota(jnp.int32, (8, 128), 0)
    lane = lax.broadcasted_iota(jnp.int32, (8, 128), 1)
    gram = jnp.zeros((8, 128), jnp.float32)
    for c in range(CHUNKS):
        for p in (0, 1, 2, 6, 7, 8):
            arrive(two_group, p, c)

        def second(f, gram):
            u = sides(buf_two, f)
            s, t = source[f], once[f]
            for k, (x, y) in enumerate(((s, s), (s, t), (t, t), (s, u), (t, u), (u, u))):
                value = jnp.sum(jnp.sum(x * y, axis=0, keepdims=True), axis=1, keepdims=True)
                gram = gram + jnp.where((row == k) & (lane == f), value, 0.0)
            return gram

        gram = lax.fori_loop(c * step, (c + 1) * step, second, gram)

    def reduce_over(gram, slots, send, recv, count, peer):
        slots[0] = gram
        copies = []
        for d in range(1, count):
            copy = pltpu.make_async_remote_copy(
                src_ref=slots.at[0],
                dst_ref=slots.at[d],
                send_sem=send.at[d],
                recv_sem=recv.at[d],
                device_id=peer(d),
                device_id_type=pl.DeviceIdType.MESH,
            )
            copy.start()
            copies.append(copy)
        for d, copy in enumerate(copies):
            copy.wait_recv()
            gram = gram + slots[d + 1]
        for copy in copies:
            copy.wait_send()
        return gram

    gram = reduce_over(gram, gram_x, x_send, x_recv, nx, lambda d: (lax.rem(i + d, nx), j))
    gram = reduce_over(gram, gram_y, y_send, y_recv, ny, lambda d: (i, lax.rem(j + d, ny)))
    gram_out[...] = gram
    finish_sends(geo_group, 1)
    finish_sends(one_group, CHUNKS)
    finish_sends(two_group, CHUNKS)


def local(
    incident,
    positions,
    nbr_part,
    nbr_slot,
    nbr_count,
    cluster_id,
    mie,
    to_waves,
    from_waves,
    to_cluster,
    cluster_waves,
    centers,
):
    bead_count = incident.shape[2]
    field_count = incident.shape[3]
    coef_width = incident.shape[4]
    wave_count = to_waves.shape[2]
    forward_matrix = block_matrix(to_waves)
    back_matrix = block_matrix(from_waves)
    source = times_phase(jnp.transpose(incident[0, 0], (1, 0, 2)), mie[0], mie[1])
    own_pos = positions[0, 0]
    flat_index = nbr_part[0, 0] * bead_count + nbr_slot[0, 0]
    slots = jnp.arange(flat_index.shape[1], dtype=jnp.int32)
    flat_index = jnp.where(slots[None, :] < nbr_count[0, 0][:, None], flat_index, -1)
    flat_index = jnp.transpose(flat_index)
    flat_index = jnp.concatenate([flat_index, flat_index], axis=1)
    rows = jnp.arange(9 * bead_count, dtype=jnp.int32)
    times = jnp.sum((flat_index[:, None, :] == rows[None, :, None]).astype(jnp.float32), axis=0)
    times = times.reshape(9, bead_count, 2 * bead_count)
    dirs = jnp.pad(sphere_grid(WAVE_LAT, WAVE_LON), ((0, 5), (0, 0)))
    column_pos = jnp.pad(jnp.transpose(own_pos), ((0, 0), (0, 125)))
    row_pos = jnp.pad(jnp.concatenate([own_pos, own_pos], axis=1), ((0, 5), (0, 0)))
    mie_rows = jnp.stack(
        [jnp.concatenate([mie[0], mie[0]]), jnp.concatenate([-mie[1], mie[1]])]
    )
    mie_rows = jnp.pad(mie_rows, ((0, 6), (0, 0)))
    nx, ny = lax.axis_size("gx"), lax.axis_size("gy")
    vmem = pl.BlockSpec(memory_space=pltpu.VMEM)
    dma = pltpu.SemaphoreType.DMA
    blocks = (field_count, 9, bead_count, coef_width)
    once, gram = pl.pallas_call(
        functools.partial(krylov_kernel, nx, ny),
        out_shape=(
            jax.ShapeDtypeStruct((field_count, bead_count, coef_width), jnp.float32),
            jax.ShapeDtypeStruct((8, 128), jnp.float32),
        ),
        in_specs=[vmem] * 8,
        out_specs=(vmem, vmem),
        scratch_shapes=[
            pltpu.VMEM(blocks, jnp.bfloat16),
            pltpu.VMEM(blocks, jnp.bfloat16),
            pltpu.VMEM((9, bead_count, 128), jnp.float32),
            pltpu.VMEM((9, bead_count, wave_count), jnp.float32),
            pltpu.VMEM((9, bead_count, wave_count), jnp.float32),
            pltpu.VMEM((9, bead_count, 2 * bead_count), jnp.bfloat16),
            pltpu.VMEM((field_count, 2 * bead_count, 2 * wave_count), jnp.float32),
            pltpu.VMEM((nx, 8, 128), jnp.float32),
            pltpu.VMEM((ny, 8, 128), jnp.float32),
            dma((8, 1)),
            dma((9, 1)),
            dma((8, CHUNKS)),
            dma((9, CHUNKS)),
            dma((8, CHUNKS)),
            dma((9, CHUNKS)),
            dma((nx,)),
            dma((nx,)),
            dma((ny,)),
            dma((ny,)),
        ],
        compiler_params=pltpu.CompilerParams(
            collective_id=0, has_side_effects=True, vmem_limit_bytes=40 * 1024 * 1024
        ),
        name="krylov",
    )(source, column_pos, row_pos, times, dirs, forward_matrix, back_matrix, mie_rows)
    w_source, w_once = weights(gram[:, :field_count])
    answer = w_source[:, None, None] * source + w_once[:, None, None] * once

    cluster_dirs = sphere_grid(CLUSTER_LAT, CLUSTER_LON)
    samples = jnp.einsum("fbc,cq->fbq", answer, block_matrix(to_cluster), precision=HI)
    bead_ids = cluster_id[0, 0]
    cluster_total = centers.shape[0]
    one_hot = (bead_ids[:, None] == jnp.arange(cluster_total, dtype=jnp.int32)[None, :]).astype(
        jnp.float32
    )
    bead_centre = jnp.dot(one_hot, centers, precision=HI)
    turn = angles(own_pos - jnp.transpose(bead_centre), cluster_dirs)
    shifted = times_phase(samples, jnp.cos(turn), jnp.sin(turn))
    span_y = lax.axis_size("gy")
    code = (bead_ids // span_y - lax.axis_index("gx")) * 2 + (
        bead_ids % span_y - lax.axis_index("gy")
    )
    hot = (jnp.arange(4, dtype=jnp.int32)[:, None] == code[None, :]).astype(jnp.float32)
    part = jnp.einsum("kb,fbq->kfq", hot, shifted, precision=HI)
    part = part.reshape(2, 2, field_count, -1)
    section = part[:, 0] + shift(part[:, 1], "gy", 1)
    own = section[0] + shift(section[1], "gx", 1)
    half = own.shape[1] // 2
    halves = jnp.concatenate([own[:, :half], own[:, half:]], axis=0)
    by_real = jnp.dot(halves, cluster_waves[0], precision=HI)
    by_imag = jnp.dot(halves, cluster_waves[1], precision=HI)
    expansions = jnp.concatenate(
        [
            by_real[:field_count] - by_imag[field_count:],
            by_imag[:field_count] + by_real[field_count:],
        ],
        axis=1,
    )
    return (jnp.transpose(answer, (1, 0, 2))[None, None], expansions[None])


def solution(mesh):
    in_specs = (
        P("gx", "gy", None, None, None),
        P("gx", "gy", None, None),
        P("gx", "gy", None, None),
        P("gx", "gy", None, None),
        P("gx", "gy", None),
        P("gx", "gy", None),
        P(),
        P(),
        P(),
        P(),
        P(),
        P(),
    )
    out_specs = (P("gx", "gy", None, None, None), P(("gx", "gy"), None, None))
    return jax.shard_map(local, mesh=mesh, in_specs=in_specs, out_specs=out_specs, check_vma=False)
```

```python
import functools
import math

import jax
import jax.numpy as jnp
from jax import lax
from jax.experimental import pallas as pl
from jax.experimental.pallas import tpu as pltpu
from jax.sharding import PartitionSpec as P

WAVE_LAT = 8
WAVE_LON = 16
CLUSTER_LAT = 16
CLUSTER_LON = 32
WAVENUMBER = 3.0
EPS = 1e-06


def sphere_grid(cycle_count, cycle_size):
    polar = (jnp.arange(cycle_count, dtype=jnp.float32) + 0.5) * (math.pi / cycle_count)
    cycle_index = jnp.arange(cycle_size, dtype=jnp.float32)
    stagger = 0.5 * (jnp.arange(cycle_count, dtype=jnp.int32) % 2).astype(jnp.float32)
    azimuth = (cycle_index[None, :] + stagger[:, None]) * (2.0 * math.pi / cycle_size)
    height = jnp.cos(polar)[:, None] * jnp.ones_like(azimuth)
    radius = jnp.sin(polar)[:, None]
    return jnp.stack(
        [
            (radius * jnp.cos(azimuth)).reshape(-1),
            (radius * jnp.sin(azimuth)).reshape(-1),
            height.reshape(-1),
        ]
    )


def block_matrix(pair):
    top_half = jnp.concatenate([pair[0], pair[1]], axis=1)
    lower_half = jnp.concatenate([-pair[1], pair[0]], axis=1)
    return jnp.concatenate([top_half, lower_half], axis=0)


def times_phase(values, cos_part, sin_part):
    half_width = values.shape[-1] // 2
    real_part = values[..., :half_width]
    imag_part = values[..., half_width:]
    return jnp.concatenate(
        [real_part * cos_part - imag_part * sin_part, real_part * sin_part + imag_part * cos_part],
        axis=-1,
    )


def weights(gram):
    ss, st, tt, su, tu, uu = [gram[k] for k in range(6)]
    beta2 = ss + EPS
    beta = jnp.sqrt(beta2)
    h11 = (ss - st) / beta2
    c = (st + EPS) / beta2
    rest = jnp.maximum((c * c * ss - 2.0 * c * st + tt) / beta2, 0.0)
    h21 = jnp.sqrt(rest + EPS)
    r = -1.0 / (beta * h21)
    p = -c * r
    h12 = (p * ss + (r - p) * st - r * su) / beta
    h22 = p * (p * ss + (r - p) * st - r * su) + r * (p * st + (r - p) * tt - r * tu)
    a = p - h12 / beta - h22 * p
    b = r - p - h22 * r
    g = -r
    q = a * a * ss + b * b * tt + g * g * uu + 2.0 * (a * b * st + a * g * su + b * g * tu)
    q = jnp.maximum(q, 0.0) + EPS
    gram_first = h11 * h11 + h21 * h21
    gram_cross = h11 * h12 + h21 * h22
    gram_second = h12 * h12 + h22 * h22 + q
    minor = h11 * h22 - h21 * h12
    det = minor * minor + q * gram_first
    y1 = beta * (gram_second * h11 - gram_cross * h12) / det
    y2 = beta * (gram_first * h12 - gram_cross * h11) / det
    return y1 / beta + y2 * p, y2 * r


CHUNKS = 2
SHIFTS = [(dx, dy) for dx in (-1, 0, 1) for dy in (-1, 0, 1)]


def krylov_kernel(
    nx,
    ny,
    source,
    column_pos,
    row_pos,
    times,
    dirs,
    forward_matrix,
    back_matrix,
    mie_rows,
    to_cluster,
    cluster_dirs,
    cluster_waves,
    answer,
    expansion,
    once,
    buf_one,
    buf_two,
    geo,
    turn_cos,
    turn_sin,
    weight,
    weight_rows,
    total,
    tc_high,
    tc_low,
    cl_cos,
    cl_sin,
    cl_samples,
    parts,
    weight_cols,
    waves,
    waves_high,
    waves_low,
    cl_send,
    cl_from_y,
    cl_forward,
    cl_from_x,
    gram_x,
    gram_y,
    geo_send,
    geo_recv,
    one_send,
    one_recv,
    two_send,
    two_recv,
    x_send,
    x_recv,
    y_send,
    y_recv,
    waves_sem,
    cl_sems,
):
    i, j = lax.axis_index("gx"), lax.axis_index("gy")
    fields, beads, width = source.shape
    wide = turn_cos.shape[2]
    step = fields // CHUNKS
    waves_copy = pltpu.make_async_copy(cluster_waves, waves, waves_sem)
    waves_copy.start()

    def loop(first, last, body, carry, size=4):
        def several(k, carry):
            for u in range(size):
                carry = body(first + k * size + u, carry)
            return carry

        return lax.fori_loop(0, (last - first) // size, several, carry)

    def split(value):
        high = value.astype(jnp.bfloat16)
        return high, (value - high.astype(jnp.float32)).astype(jnp.bfloat16)

    def dot(a, b):
        return jnp.dot(a, b, preferred_element_type=jnp.float32)

    def present(dx, dy):
        return (i + dx >= 0) & (i + dx < nx) & (j + dy >= 0) & (j + dy < ny)

    def piece(buf, p, c):
        if len(buf.shape) == 3:
            return buf.at[p]
        return buf.at[pl.ds(c * step, step), p]

    def make(buf, send, recv, slot, src, dst, c, dx, dy):
        return pltpu.make_async_remote_copy(
            src_ref=piece(buf, src, c),
            dst_ref=piece(buf, dst, c),
            send_sem=send.at[slot, c],
            recv_sem=recv.at[dst, c],
            device_id=(i + dx, j + dy),
            device_id_type=pl.DeviceIdType.MESH,
        )

    own_routes = [(0, 4, 3, 0, 1), (1, 4, 5, 0, -1), (2, 4, 1, 1, 0), (3, 4, 7, -1, 0)]
    low_routes = [(4, 3, 0, 1, 0), (5, 3, 6, -1, 0)]
    high_routes = [(6, 5, 2, 1, 0), (7, 5, 8, -1, 0)]

    def guarded(route):
        ok = present(route[3], route[4])
        if route[1] == 3:
            ok = ok & (j > 0)
        if route[1] == 5:
            ok = ok & (j < ny - 1)
        return pl.when(ok)

    def start(group, routes, c):
        for route in routes:

            @guarded(route)
            def _(route=route):
                slot, src, dst, dx, dy = route
                make(*group, slot, src, dst, c, dx, dy).start()

    def finish_sends(group, count):
        for c in range(count):
            for route in own_routes + low_routes + high_routes:

                @guarded(route)
                def _(route=route, c=c):
                    slot, src, dst, dx, dy = route
                    make(*group, slot, src, dst, c, dx, dy).wait_send()

    def arrive(group, p, c):
        dx, dy = SHIFTS[p]
        via = (dx, 0) if dx != 0 else (0, dy)

        @pl.when(present(dx, dy))
        def _():
            make(*group, 0, 4, p, c, via[0], via[1]).wait_recv()

    def forward(group, c):
        arrive(group, 3, c)
        start(group, low_routes, c)
        arrive(group, 5, c)
        start(group, high_routes, c)

    geo_group = (geo, geo_send, geo_recv)
    one_group = (buf_one, one_send, one_recv)
    two_group = (buf_two, two_send, two_recv)

    barrier = pltpu.get_barrier_semaphore()
    for d in range(1, nx):
        pl.semaphore_signal(
            barrier,
            inc=1,
            device_id=(lax.rem(i + d, nx), j),
            device_id_type=pl.DeviceIdType.MESH,
        )
    for d in range(1, ny):
        pl.semaphore_signal(
            barrier,
            inc=1,
            device_id=(i, lax.rem(j + d, ny)),
            device_id_type=pl.DeviceIdType.MESH,
        )
    geo[4] = column_pos[...]

    def to_low(f, carry):
        buf_one[f, 4] = source[f].astype(jnp.bfloat16)
        return carry

    lax.fori_loop(0, fields, to_low, 0)
    for p, (dx, dy) in enumerate(SHIFTS):

        @pl.when(jnp.logical_not(present(dx, dy)))
        def _(p=p):
            geo[p] = jnp.zeros(geo.shape[1:], geo.dtype)

            def clear(f, carry):
                buf_one[f, p] = jnp.zeros((beads, width), jnp.bfloat16)
                buf_two[f, p] = jnp.zeros((beads, width), jnp.bfloat16)
                return carry

            lax.fori_loop(0, fields, clear, 0)

    pl.semaphore_wait(barrier, nx + ny - 2)

    start(geo_group, own_routes, 0)
    for c in range(CHUNKS):
        start(one_group, own_routes, c)
    forward(geo_group, 0)

    def geometry(p):
        pos = geo[p]
        along = (
            pos[:, 0:1] * dirs[0:1, :] + pos[:, 1:2] * dirs[1:2, :] + pos[:, 2:3] * dirs[2:3, :]
        )
        angle = WAVENUMBER * along
        turn_cos[p] = jnp.cos(angle)
        turn_sin[p] = jnp.sin(angle)
        ex = row_pos[0:1, :] - pos[:, 0:1]
        ey = row_pos[1:2, :] - pos[:, 1:2]
        ez = row_pos[2:3, :] - pos[:, 2:3]
        dist = jnp.sqrt(ex * ex + ey * ey + ez * ez)
        full = times[p] / (1.0 + dist)
        high = full.astype(jnp.bfloat16).astype(jnp.float32)
        lane = lax.broadcasted_iota(jnp.int32, full.shape, 1)
        weight_rows[p] = jnp.where(lane < beads, high, full - high)

    def turn_weights(g):
        rows = weight_rows[3 * g : 3 * g + 3].reshape(3 * beads, 2 * beads)
        weight[g] = jnp.transpose(rows).astype(jnp.bfloat16)

    cl_wide = cl_cos.shape[1]

    def cluster_setup():
        along = (
            column_pos[:, 3:4] * cluster_dirs[0:1, :]
            + column_pos[:, 4:5] * cluster_dirs[1:2, :]
            + column_pos[:, 5:6] * cluster_dirs[2:3, :]
        )
        angle = WAVENUMBER * along
        cl_cos[...] = jnp.cos(angle)
        cl_sin[...] = jnp.sin(angle)
        half = width // 2
        real_high, real_low = split(to_cluster[0])
        imag_high, imag_low = split(to_cluster[1])
        for ref, real, imag in ((tc_high, real_high, imag_high), (tc_low, real_low, imag_low)):
            ref[0:half, 0:cl_wide] = real
            ref[0:half, cl_wide : 2 * cl_wide] = imag
            ref[half:width, 0:cl_wide] = -imag
            ref[half:width, cl_wide : 2 * cl_wide] = real

    def cluster_parts(values, kind, c):
        high, low = split(values[pl.ds(c * step, step)].reshape(step * beads, width))
        smp = dot(high, tc_high[...]) + dot(low, tc_high[...]) + dot(high, tc_low[...])
        cl_samples[...] = smp.reshape(step, beads, 2 * cl_wide)

        def body(f, carry):
            re, im = cl_samples[f, :, :cl_wide], cl_samples[f, :, cl_wide:]
            co, si = cl_cos[...], cl_sin[...]
            real = re * co - im * si
            imag = re * si + im * co
            for k in range(4):
                hot = column_pos[:, 8 + k : 9 + k]
                spot = pl.ds(c * step + f, 1)
                parts[kind, k, spot, 0:cl_wide] = jnp.sum(real * hot, axis=0, keepdims=True)
                parts[kind, k, spot, cl_wide : 2 * cl_wide] = jnp.sum(
                    imag * hot, axis=0, keepdims=True
                )
            return carry

        lax.fori_loop(0, step, body, 0)

    geometry(4)
    for p in (3, 5):
        geometry(p)
    turn_weights(1)
    cluster_setup()
    for c in range(CHUNKS):
        forward(one_group, c)
        cluster_parts(source, 0, c)
    for p in (0, 1, 2, 6, 7, 8):
        arrive(geo_group, p, 0)
        geometry(p)
    turn_weights(0)
    turn_weights(2)

    def gathered(buf, f, first, count):
        rows = count * beads
        spot = pl.ds(first, count)
        low = buf[f, spot].reshape(rows, width)
        smp = jnp.dot(low, forward_matrix[...], preferred_element_type=jnp.float32)
        re, im = smp[:, :wide], smp[:, wide:]
        co = turn_cos[spot].reshape(rows, wide)
        si = turn_sin[spot].reshape(rows, wide)
        turned = jnp.concatenate(
            [
                (re * co + im * si).astype(jnp.bfloat16),
                (im * co - re * si).astype(jnp.bfloat16),
            ],
            axis=1,
        )
        return dot(weight[first // 3], turned)

    def back_turn(acc):
        inc = acc[:beads] + acc[beads:]
        re, im = inc[:, :wide], inc[:, wide:]
        co, si = turn_cos[4], turn_sin[4]
        inc = jnp.concatenate([re * co - im * si, re * si + im * co], axis=1)
        high = inc.astype(jnp.bfloat16)
        low = (inc - high.astype(jnp.float32)).astype(jnp.bfloat16)
        back = jnp.dot(
            jnp.concatenate([high, low], axis=0),
            back_matrix[...],
            preferred_element_type=jnp.float32,
        )
        back = back[:beads] + back[beads:]
        return back * mie_rows[0:1, :] + pltpu.roll(back, width // 2, 1) * mie_rows[1:2, :]

    def middle(buf):
        def body(f, carry):
            total[f] = gathered(buf, f, 3, 3)
            return carry

        loop(0, fields, body, 0)

    def sides(buf, f):
        return back_turn(total[f] + gathered(buf, f, 0, 3) + gathered(buf, f, 6, 3))

    middle(buf_one)
    for c in range(CHUNKS):
        for p in (0, 1, 2, 6, 7, 8):
            arrive(one_group, p, c)

        def first(f, carry):
            value = sides(buf_one, f)
            once[f] = value
            buf_two[f, 4] = value.astype(jnp.bfloat16)
            return carry

        loop(c * step, (c + 1) * step, first, 0)
        start(two_group, own_routes, c)

    for c in range(CHUNKS):
        cluster_parts(once, 1, c)
        forward(two_group, c)
    middle(buf_two)
    waves_copy.wait()

    def halve(k, carry):
        spot = pl.ds(k * 64, 64)
        for part in range(2):
            high, low = split(waves[part, spot, :])
            waves_high[part, spot, :] = high
            waves_low[part, spot, :] = low
        return carry

    lax.fori_loop(0, waves.shape[1] // 64, halve, 0)

    row = lax.broadcasted_iota(jnp.int32, (8, 128), 0)
    lane = lax.broadcasted_iota(jnp.int32, (8, 128), 1)
    gram = jnp.zeros((8, 128), jnp.float32)
    for c in range(CHUNKS):
        for p in (0, 1, 2, 6, 7, 8):
            arrive(two_group, p, c)

        def second(f, gram):
            u = sides(buf_two, f)
            s, t = source[f], once[f]
            for k, (x, y) in enumerate(((s, s), (s, t), (t, t), (s, u), (t, u), (u, u))):
                value = jnp.sum(jnp.sum(x * y, axis=0, keepdims=True), axis=1, keepdims=True)
                gram = gram + jnp.where((row == k) & (lane == f), value, 0.0)
            return gram

        gram = loop(c * step, (c + 1) * step, second, gram, 2)

    def reduce_over(gram, slots, send, recv, count, peer):
        slots[0] = gram
        copies = []
        for d in range(1, count):
            copy = pltpu.make_async_remote_copy(
                src_ref=slots.at[0],
                dst_ref=slots.at[d],
                send_sem=send.at[d],
                recv_sem=recv.at[d],
                device_id=peer(d),
                device_id_type=pl.DeviceIdType.MESH,
            )
            copy.start()
            copies.append(copy)
        for d, copy in enumerate(copies):
            copy.wait_recv()
            gram = gram + slots[d + 1]
        for copy in copies:
            copy.wait_send()
        return gram

    gram = reduce_over(gram, gram_x, x_send, x_recv, nx, lambda d: (lax.rem(i + d, nx), j))
    gram = reduce_over(gram, gram_y, y_send, y_recv, ny, lambda d: (i, lax.rem(j + d, ny)))
    w_source, w_once = weights([gram[k : k + 1] for k in range(6)])
    diagonal = lax.broadcasted_iota(jnp.int32, (fields, 128), 0) == lax.broadcasted_iota(
        jnp.int32, (fields, 128), 1
    )
    columns = []
    for k, w in enumerate((w_source, w_once)):
        column = jnp.sum(jnp.where(diagonal, w, 0.0), axis=1, keepdims=True)
        columns.append(column)
        weight_cols[k] = jnp.broadcast_to(column, (fields, 128))
    mixed = [parts[0, k] * columns[0] + parts[1, k] * columns[1] for k in range(4)]
    cl_send[0] = mixed[1]
    cl_send[1] = mixed[3]

    def move(src, dst, base, dx, dy):
        return pltpu.make_async_remote_copy(
            src_ref=src,
            dst_ref=dst,
            send_sem=cl_sems.at[base],
            recv_sem=cl_sems.at[base + 1],
            device_id=(i + dx, j + dy),
            device_id_type=pl.DeviceIdType.MESH,
        )

    @pl.when(j < ny - 1)
    def _():
        move(cl_send, cl_from_y, 0, 0, 1).start()

    @pl.when(j == 0)
    def _():
        cl_from_y[...] = jnp.zeros(cl_from_y.shape, jnp.float32)

    @pl.when(i == 0)
    def _():
        cl_from_x[...] = jnp.zeros(cl_from_x.shape, jnp.float32)

    @pl.when(j > 0)
    def _():
        move(cl_send, cl_from_y, 0, 0, -1).wait_recv()

    cl_forward[...] = mixed[2] + cl_from_y[1]

    @pl.when(i < nx - 1)
    def _():
        move(cl_forward, cl_from_x, 2, 1, 0).start()

    def combine(f, carry):
        ws = weight_cols[0, pl.ds(f, 1), :]
        wo = weight_cols[1, pl.ds(f, 1), :]
        answer[f] = source[f] * ws + once[f] * wo
        return carry

    lax.fori_loop(0, fields, combine, 0)

    @pl.when(i > 0)
    def _():
        move(cl_forward, cl_from_x, 2, -1, 0).wait_recv()

    own = mixed[0] + cl_from_y[0] + cl_from_x[...]
    halves = jnp.concatenate([own[:, :cl_wide], own[:, cl_wide:]], axis=0)
    high, low = split(halves)
    by = [
        dot(high, waves_high[k]) + dot(low, waves_high[k]) + dot(high, waves_low[k])
        for k in range(2)
    ]
    expansion[0] = by[0][:fields] - by[1][fields:]
    expansion[1] = by[1][:fields] + by[0][fields:]

    @pl.when(j < ny - 1)
    def _():
        move(cl_send, cl_from_y, 0, 0, 1).wait_send()

    @pl.when(i < nx - 1)
    def _():
        move(cl_forward, cl_from_x, 2, 1, 0).wait_send()

    finish_sends(geo_group, 1)
    finish_sends(one_group, CHUNKS)
    finish_sends(two_group, CHUNKS)


def local(
    incident,
    positions,
    nbr_part,
    nbr_slot,
    nbr_count,
    cluster_id,
    mie,
    to_waves,
    from_waves,
    to_cluster,
    cluster_waves,
    centers,
):
    bead_count = incident.shape[2]
    field_count = incident.shape[3]
    coef_width = incident.shape[4]
    wave_count = to_waves.shape[2]
    forward_matrix = block_matrix(to_waves)
    back_matrix = block_matrix(from_waves)
    source = times_phase(jnp.transpose(incident[0, 0], (1, 0, 2)), mie[0], mie[1])
    own_pos = positions[0, 0]
    flat_index = nbr_part[0, 0] * bead_count + nbr_slot[0, 0]
    slots = jnp.arange(flat_index.shape[1], dtype=jnp.int32)
    flat_index = jnp.where(slots[None, :] < nbr_count[0, 0][:, None], flat_index, -1)
    flat_index = jnp.transpose(flat_index)
    flat_index = jnp.concatenate([flat_index, flat_index], axis=1)
    rows = jnp.arange(9 * bead_count, dtype=jnp.int32)
    times = jnp.sum((flat_index[:, None, :] == rows[None, :, None]).astype(jnp.float32), axis=0)
    times = times.reshape(9, bead_count, 2 * bead_count)
    dirs = jnp.pad(sphere_grid(WAVE_LAT, WAVE_LON), ((0, 5), (0, 0)))
    bead_ids = cluster_id[0, 0]
    cluster_total = centers.shape[0]
    one_hot = (bead_ids[:, None] == jnp.arange(cluster_total, dtype=jnp.int32)[None, :]).astype(
        jnp.float32
    )
    bead_centre = jnp.sum(one_hot[:, :, None] * centers[None], axis=1)
    span_y = lax.axis_size("gy")
    code = (bead_ids // span_y - lax.axis_index("gx")) * 2 + (
        bead_ids % span_y - lax.axis_index("gy")
    )
    hot = (code[:, None] == jnp.arange(4, dtype=jnp.int32)[None, :]).astype(jnp.float32)
    pos_t = jnp.transpose(own_pos)
    column_pos = jnp.concatenate(
        [pos_t, pos_t - bead_centre, jnp.zeros((bead_count, 2), jnp.float32), hot], axis=1
    )
    column_pos = jnp.pad(column_pos, ((0, 0), (0, 116)))
    cluster_dirs = jnp.pad(sphere_grid(CLUSTER_LAT, CLUSTER_LON), ((0, 5), (0, 0)))
    cl_wide = to_cluster.shape[2]
    cl_coef = cluster_waves.shape[2]
    row_pos = jnp.pad(jnp.concatenate([own_pos, own_pos], axis=1), ((0, 5), (0, 0)))
    mie_rows = jnp.stack(
        [jnp.concatenate([mie[0], mie[0]]), jnp.concatenate([-mie[1], mie[1]])]
    )
    mie_rows = jnp.pad(mie_rows, ((0, 6), (0, 0)))
    nx, ny = lax.axis_size("gx"), lax.axis_size("gy")
    vmem = pl.BlockSpec(memory_space=pltpu.VMEM)
    dma = pltpu.SemaphoreType.DMA
    blocks = (field_count, 9, bead_count, coef_width)
    answer, expansion = pl.pallas_call(
        functools.partial(krylov_kernel, nx, ny),
        out_shape=(
            jax.ShapeDtypeStruct((field_count, bead_count, coef_width), jnp.float32),
            jax.ShapeDtypeStruct((2, field_count, cl_coef), jnp.float32),
        ),
        in_specs=[vmem] * 10 + [pl.BlockSpec(memory_space=pl.ANY)],
        out_specs=(vmem, vmem),
        scratch_shapes=[
            pltpu.VMEM((field_count, bead_count, coef_width), jnp.float32),
            pltpu.VMEM(blocks, jnp.bfloat16),
            pltpu.VMEM(blocks, jnp.bfloat16),
            pltpu.VMEM((9, bead_count, 128), jnp.float32),
            pltpu.VMEM((9, bead_count, wave_count), jnp.float32),
            pltpu.VMEM((9, bead_count, wave_count), jnp.float32),
            pltpu.VMEM((3, 2 * bead_count, 3 * bead_count), jnp.bfloat16),
            pltpu.VMEM((9, bead_count, 2 * bead_count), jnp.float32),
            pltpu.VMEM((field_count, 2 * bead_count, 2 * wave_count), jnp.float32),
            pltpu.VMEM((coef_width, 2 * cl_wide), jnp.bfloat16),
            pltpu.VMEM((coef_width, 2 * cl_wide), jnp.bfloat16),
            pltpu.VMEM((bead_count, cl_wide), jnp.float32),
            pltpu.VMEM((bead_count, cl_wide), jnp.float32),
            pltpu.VMEM((field_count // CHUNKS, bead_count, 2 * cl_wide), jnp.float32),
            pltpu.VMEM((2, 4, field_count, 2 * cl_wide), jnp.float32),
            pltpu.VMEM((2, field_count, 128), jnp.float32),
            pltpu.VMEM(cluster_waves.shape, jnp.float32),
            pltpu.VMEM(cluster_waves.shape, jnp.bfloat16),
            pltpu.VMEM(cluster_waves.shape, jnp.bfloat16),
            pltpu.VMEM((2, field_count, 2 * cl_wide), jnp.float32),
            pltpu.VMEM((2, field_count, 2 * cl_wide), jnp.float32),
            pltpu.VMEM((field_count, 2 * cl_wide), jnp.float32),
            pltpu.VMEM((field_count, 2 * cl_wide), jnp.float32),
            pltpu.VMEM((nx, 8, 128), jnp.float32),
            pltpu.VMEM((ny, 8, 128), jnp.float32),
            dma((8, 1)),
            dma((9, 1)),
            dma((8, CHUNKS)),
            dma((9, CHUNKS)),
            dma((8, CHUNKS)),
            dma((9, CHUNKS)),
            dma((nx,)),
            dma((nx,)),
            dma((ny,)),
            dma((ny,)),
            dma,
            dma((4,)),
        ],
        compiler_params=pltpu.CompilerParams(
            collective_id=0, has_side_effects=True, vmem_limit_bytes=40 * 1024 * 1024
        ),
        name="krylov",
    )(
        source,
        column_pos,
        row_pos,
        times,
        dirs,
        forward_matrix,
        back_matrix,
        mie_rows,
        to_cluster,
        cluster_dirs,
        cluster_waves,
    )
    expansions = jnp.concatenate([expansion[0], expansion[1]], axis=1)
    return (jnp.transpose(answer, (1, 0, 2))[None, None], expansions[None])


def solution(mesh):
    in_specs = (
        P("gx", "gy", None, None, None),
        P("gx", "gy", None, None),
        P("gx", "gy", None, None),
        P("gx", "gy", None, None),
        P("gx", "gy", None),
        P("gx", "gy", None),
        P(),
        P(),
        P(),
        P(),
        P(),
        P(),
    )
    out_specs = (P("gx", "gy", None, None, None), P(("gx", "gy"), None, None))
    return jax.shard_map(local, mesh=mesh, in_specs=in_specs, out_specs=out_specs, check_vma=False)
```

```python
import functools
import math

import jax
import jax.numpy as jnp
import numpy as np
from jax import lax
from jax.experimental import pallas as pl
from jax.experimental.pallas import tpu as pltpu
from jax.sharding import PartitionSpec as P

WAVE_LAT = 8
WAVE_LON = 16
CLUSTER_LAT = 16
CLUSTER_LON = 32
WAVENUMBER = 3.0
EPS = 1e-06


def sphere_grid(cycle_count, cycle_size):
    polar = (np.arange(cycle_count) + 0.5) * (math.pi / cycle_count)
    stagger = 0.5 * (np.arange(cycle_count) % 2)
    azimuth = (np.arange(cycle_size)[None, :] + stagger[:, None]) * (2.0 * math.pi / cycle_size)
    height = np.cos(polar)[:, None] * np.ones_like(azimuth)
    radius = np.sin(polar)[:, None]
    grid = np.zeros((8, cycle_count * cycle_size), np.float32)
    grid[0] = (radius * np.cos(azimuth)).reshape(-1)
    grid[1] = (radius * np.sin(azimuth)).reshape(-1)
    grid[2] = height.reshape(-1)
    return grid


def weights(gram):
    ss, st, tt, su, tu, uu = [gram[k] for k in range(6)]
    beta2 = ss + EPS
    beta = jnp.sqrt(beta2)
    h11 = (ss - st) / beta2
    c = (st + EPS) / beta2
    rest = jnp.maximum((c * c * ss - 2.0 * c * st + tt) / beta2, 0.0)
    h21 = jnp.sqrt(rest + EPS)
    r = -1.0 / (beta * h21)
    p = -c * r
    h12 = (p * ss + (r - p) * st - r * su) / beta
    h22 = p * (p * ss + (r - p) * st - r * su) + r * (p * st + (r - p) * tt - r * tu)
    a = p - h12 / beta - h22 * p
    b = r - p - h22 * r
    g = -r
    q = a * a * ss + b * b * tt + g * g * uu + 2.0 * (a * b * st + a * g * su + b * g * tu)
    q = jnp.maximum(q, 0.0) + EPS
    gram_first = h11 * h11 + h21 * h21
    gram_cross = h11 * h12 + h21 * h22
    gram_second = h12 * h12 + h22 * h22 + q
    minor = h11 * h22 - h21 * h12
    det = minor * minor + q * gram_first
    y1 = beta * (gram_second * h11 - gram_cross * h12) / det
    y2 = beta * (gram_first * h12 - gram_cross * h11) / det
    return y1 / beta + y2 * p, y2 * r


CHUNKS = 2
SHIFTS = [(dx, dy) for dx in (-1, 0, 1) for dy in (-1, 0, 1)]


def krylov_kernel(
    nx,
    ny,
    incident,
    column_pos,
    row_pos,
    times,
    dirs,
    to_waves,
    from_waves,
    mie,
    to_cluster,
    cluster_dirs,
    cluster_waves,
    answer,
    expansion,
    source,
    forward_matrix,
    back_matrix,
    mie_rows,
    once,
    buf_one,
    buf_two,
    geo,
    turn_cos,
    turn_sin,
    weight,
    weight_rows,
    total,
    tc_high,
    tc_low,
    cl_cos,
    cl_sin,
    cl_samples,
    parts,
    weight_cols,
    waves,
    waves_high,
    waves_low,
    cl_send,
    cl_from_y,
    cl_forward,
    cl_from_x,
    gram_x,
    gram_y,
    geo_send,
    geo_recv,
    one_send,
    one_recv,
    two_send,
    two_recv,
    x_send,
    x_recv,
    y_send,
    y_recv,
    waves_sem,
    cl_sems,
):
    i, j = lax.axis_index("gx"), lax.axis_index("gy")
    fields, beads, width = source.shape
    wide = turn_cos.shape[2]
    step = fields // CHUNKS
    wave_rows = cluster_waves.shape[0]
    waves_copy = pltpu.make_async_copy(cluster_waves, waves.at[pl.ds(0, wave_rows)], waves_sem)
    waves_copy.start()

    def loop(first, last, body, carry, size=4):
        def several(k, carry):
            for u in range(size):
                carry = body(first + k * size + u, carry)
            return carry

        return lax.fori_loop(0, (last - first) // size, several, carry)

    def split(value):
        high = value.astype(jnp.bfloat16)
        return high, (value - high.astype(jnp.float32)).astype(jnp.bfloat16)

    def dot(a, b):
        return jnp.dot(a, b, preferred_element_type=jnp.float32)

    def dot_turned(a, b):
        return lax.dot_general(
            a, b, (((1,), (1,)), ((), ())), preferred_element_type=jnp.float32
        )

    def present(dx, dy):
        return (i + dx >= 0) & (i + dx < nx) & (j + dy >= 0) & (j + dy < ny)

    def piece(buf, p, c):
        if len(buf.shape) == 3:
            return buf.at[p]
        return buf.at[pl.ds(c * step, step), p]

    def make(buf, send, recv, slot, src, dst, c, dx, dy):
        return pltpu.make_async_remote_copy(
            src_ref=piece(buf, src, c),
            dst_ref=piece(buf, dst, c),
            send_sem=send.at[slot, c],
            recv_sem=recv.at[dst, c],
            device_id=(i + dx, j + dy),
            device_id_type=pl.DeviceIdType.MESH,
        )

    own_routes = [(0, 4, 3, 0, 1), (1, 4, 5, 0, -1), (2, 4, 1, 1, 0), (3, 4, 7, -1, 0)]
    low_routes = [(4, 3, 0, 1, 0), (5, 3, 6, -1, 0)]
    high_routes = [(6, 5, 2, 1, 0), (7, 5, 8, -1, 0)]

    def guarded(route):
        ok = present(route[3], route[4])
        if route[1] == 3:
            ok = ok & (j > 0)
        if route[1] == 5:
            ok = ok & (j < ny - 1)
        return pl.when(ok)

    def start(group, routes, c):
        for route in routes:

            @guarded(route)
            def _(route=route):
                slot, src, dst, dx, dy = route
                make(*group, slot, src, dst, c, dx, dy).start()

    def finish_sends(group, count):
        for c in range(count):
            for route in own_routes + low_routes + high_routes:

                @guarded(route)
                def _(route=route, c=c):
                    slot, src, dst, dx, dy = route
                    make(*group, slot, src, dst, c, dx, dy).wait_send()

    def arrive(group, p, c):
        dx, dy = SHIFTS[p]
        via = (dx, 0) if dx != 0 else (0, dy)

        @pl.when(present(dx, dy))
        def _():
            make(*group, 0, 4, p, c, via[0], via[1]).wait_recv()

    def forward(group, c):
        arrive(group, 3, c)
        start(group, low_routes, c)
        arrive(group, 5, c)
        start(group, high_routes, c)

    geo_group = (geo, geo_send, geo_recv)
    one_group = (buf_one, one_send, one_recv)
    two_group = (buf_two, two_send, two_recv)

    barrier = pltpu.get_barrier_semaphore()
    for d in range(1, nx):
        pl.semaphore_signal(
            barrier,
            inc=1,
            device_id=(lax.rem(i + d, nx), j),
            device_id_type=pl.DeviceIdType.MESH,
        )
    for d in range(1, ny):
        pl.semaphore_signal(
            barrier,
            inc=1,
            device_id=(i, lax.rem(j + d, ny)),
            device_id_type=pl.DeviceIdType.MESH,
        )
    geo[4] = column_pos[...]

    half = width // 2
    mie_rows[0:1, 0:half] = mie[0:1, :]
    mie_rows[0:1, half:width] = mie[0:1, :]
    mie_rows[1:2, 0:half] = -mie[1:2, :]
    mie_rows[1:2, half:width] = mie[1:2, :]
    for f in range(fields):
        value = incident[:, f, :]
        value = value * mie_rows[0:1, :] + pltpu.roll(value, half, 1) * mie_rows[1:2, :]
        source[f] = value
        buf_one[f, 4] = value.astype(jnp.bfloat16)
    forward_matrix[0:half, 0:wide] = to_waves[0]
    forward_matrix[0:half, wide : 2 * wide] = to_waves[1]
    forward_matrix[half:width, 0:wide] = -to_waves[1]
    forward_matrix[half:width, wide : 2 * wide] = to_waves[0]
    back_matrix[0:half, 0:wide] = from_waves[0]
    back_matrix[0:half, wide : 2 * wide] = -from_waves[1]
    back_matrix[half:width, 0:wide] = from_waves[1]
    back_matrix[half:width, wide : 2 * wide] = from_waves[0]
    waves[pl.ds(wave_rows, waves.shape[0] - wave_rows)] = jnp.zeros(
        (waves.shape[0] - wave_rows, 128), jnp.float32
    )
    for p, (dx, dy) in enumerate(SHIFTS):

        @pl.when(jnp.logical_not(present(dx, dy)))
        def _(p=p):
            geo[p] = jnp.zeros(geo.shape[1:], geo.dtype)

            def clear(f, carry):
                buf_one[f, p] = jnp.zeros((beads, width), jnp.bfloat16)
                buf_two[f, p] = jnp.zeros((beads, width), jnp.bfloat16)
                return carry

            lax.fori_loop(0, fields, clear, 0)

    pl.semaphore_wait(barrier, nx + ny - 2)

    start(geo_group, own_routes, 0)
    for c in range(CHUNKS):
        start(one_group, own_routes, c)
    forward(geo_group, 0)

    def geometry(p):
        pos = geo[p]
        along = (
            pos[:, 0:1] * dirs[0:1, :] + pos[:, 1:2] * dirs[1:2, :] + pos[:, 2:3] * dirs[2:3, :]
        )
        angle = WAVENUMBER * along
        turn_cos[p] = jnp.cos(angle)
        turn_sin[p] = jnp.sin(angle)
        ex = row_pos[0:1, :] - pos[:, 0:1]
        ey = row_pos[1:2, :] - pos[:, 1:2]
        ez = row_pos[2:3, :] - pos[:, 2:3]
        dist = jnp.sqrt(ex * ex + ey * ey + ez * ez)
        full = times[p] / (1.0 + dist)
        high = full.astype(jnp.bfloat16).astype(jnp.float32)
        lane = lax.broadcasted_iota(jnp.int32, full.shape, 1)
        weight_rows[p] = jnp.where(lane < beads, high, full - high)

    def turn_weights(g):
        rows = weight_rows[3 * g : 3 * g + 3].reshape(3 * beads, 2 * beads)
        weight[g] = jnp.transpose(rows).astype(jnp.bfloat16)

    cl_wide = cl_cos.shape[1]

    def cluster_setup():
        along = (
            column_pos[:, 3:4] * cluster_dirs[0:1, :]
            + column_pos[:, 4:5] * cluster_dirs[1:2, :]
            + column_pos[:, 5:6] * cluster_dirs[2:3, :]
        )
        angle = WAVENUMBER * along
        cl_cos[...] = jnp.cos(angle)
        cl_sin[...] = jnp.sin(angle)
        real_high, real_low = split(to_cluster[0])
        imag_high, imag_low = split(to_cluster[1])
        for ref, real, imag in ((tc_high, real_high, imag_high), (tc_low, real_low, imag_low)):
            ref[0:half, 0:cl_wide] = real
            ref[0:half, cl_wide : 2 * cl_wide] = imag
            ref[half:width, 0:cl_wide] = -imag
            ref[half:width, cl_wide : 2 * cl_wide] = real

    def cluster_parts(values, kind, c):
        high, low = split(values[pl.ds(c * step, step)].reshape(step * beads, width))
        smp = dot(high, tc_high[...]) + dot(low, tc_high[...]) + dot(high, tc_low[...])
        cl_samples[...] = smp.reshape(step, beads, 2 * cl_wide)

        def body(f, carry):
            re, im = cl_samples[f, :, :cl_wide], cl_samples[f, :, cl_wide:]
            co, si = cl_cos[...], cl_sin[...]
            real = re * co - im * si
            imag = re * si + im * co
            for k in range(4):
                hot = column_pos[:, 8 + k : 9 + k]
                spot = pl.ds(c * step + f, 1)
                parts[kind, k, spot, 0:cl_wide] = jnp.sum(real * hot, axis=0, keepdims=True)
                parts[kind, k, spot, cl_wide : 2 * cl_wide] = jnp.sum(
                    imag * hot, axis=0, keepdims=True
                )
            return carry

        lax.fori_loop(0, step, body, 0)

    geometry(4)
    for p in (3, 5):
        geometry(p)
    turn_weights(1)
    cluster_setup()
    for c in range(CHUNKS):
        forward(one_group, c)
        cluster_parts(source, 0, c)
    for p in (0, 1, 2, 6, 7, 8):
        arrive(geo_group, p, 0)
        geometry(p)
    turn_weights(0)
    turn_weights(2)

    def gathered(buf, f, first, count):
        rows = count * beads
        spot = pl.ds(first, count)
        low = buf[f, spot].reshape(rows, width)
        smp = jnp.dot(low, forward_matrix[...], preferred_element_type=jnp.float32)
        re, im = smp[:, :wide], smp[:, wide:]
        co = turn_cos[spot].reshape(rows, wide)
        si = turn_sin[spot].reshape(rows, wide)
        turned = jnp.concatenate(
            [
                (re * co + im * si).astype(jnp.bfloat16),
                (im * co - re * si).astype(jnp.bfloat16),
            ],
            axis=1,
        )
        return dot(weight[first // 3], turned)

    def back_turn(acc):
        inc = acc[:beads] + acc[beads:]
        re, im = inc[:, :wide], inc[:, wide:]
        co, si = turn_cos[4], turn_sin[4]
        inc = jnp.concatenate([re * co - im * si, re * si + im * co], axis=1)
        high = inc.astype(jnp.bfloat16)
        low = (inc - high.astype(jnp.float32)).astype(jnp.bfloat16)
        back = dot_turned(jnp.concatenate([high, low], axis=0), back_matrix[...])
        back = back[:beads] + back[beads:]
        return back * mie_rows[0:1, :] + pltpu.roll(back, width // 2, 1) * mie_rows[1:2, :]

    def middle(buf):
        def body(f, carry):
            total[f] = gathered(buf, f, 3, 3)
            return carry

        loop(0, fields, body, 0)

    def sides(buf, f):
        return back_turn(total[f] + gathered(buf, f, 0, 3) + gathered(buf, f, 6, 3))

    middle(buf_one)
    for c in range(CHUNKS):
        for p in (0, 1, 2, 6, 7, 8):
            arrive(one_group, p, c)

        def first(f, carry):
            value = sides(buf_one, f)
            once[f] = value
            buf_two[f, 4] = value.astype(jnp.bfloat16)
            return carry

        loop(c * step, (c + 1) * step, first, 0)
        start(two_group, own_routes, c)

    for c in range(CHUNKS):
        cluster_parts(once, 1, c)
        forward(two_group, c)
    middle(buf_two)
    waves_copy.wait()

    lanes = cl_wide // 128
    for block in range(lanes):
        for part in range(2):
            rows = waves_high.shape[1]
            high, low = split(waves[pl.ds(2 * block + part, rows, stride=2 * lanes), :])
            waves_high[part, :, 128 * block : 128 * block + 128] = high
            waves_low[part, :, 128 * block : 128 * block + 128] = low

    row = lax.broadcasted_iota(jnp.int32, (8, 128), 0)
    lane = lax.broadcasted_iota(jnp.int32, (8, 128), 1)
    gram = jnp.zeros((8, 128), jnp.float32)
    for c in range(CHUNKS):
        for p in (0, 1, 2, 6, 7, 8):
            arrive(two_group, p, c)

        def second(f, gram):
            u = sides(buf_two, f)
            s, t = source[f], once[f]
            for k, (x, y) in enumerate(((s, s), (s, t), (t, t), (s, u), (t, u), (u, u))):
                value = jnp.sum(jnp.sum(x * y, axis=0, keepdims=True), axis=1, keepdims=True)
                gram = gram + jnp.where((row == k) & (lane == f), value, 0.0)
            return gram

        gram = loop(c * step, (c + 1) * step, second, gram, 2)

    def reduce_over(gram, slots, send, recv, count, peer):
        slots[0] = gram
        copies = []
        for d in range(1, count):
            copy = pltpu.make_async_remote_copy(
                src_ref=slots.at[0],
                dst_ref=slots.at[d],
                send_sem=send.at[d],
                recv_sem=recv.at[d],
                device_id=peer(d),
                device_id_type=pl.DeviceIdType.MESH,
            )
            copy.start()
            copies.append(copy)
        for d, copy in enumerate(copies):
            copy.wait_recv()
            gram = gram + slots[d + 1]
        for copy in copies:
            copy.wait_send()
        return gram

    gram = reduce_over(gram, gram_x, x_send, x_recv, nx, lambda d: (lax.rem(i + d, nx), j))
    gram = reduce_over(gram, gram_y, y_send, y_recv, ny, lambda d: (i, lax.rem(j + d, ny)))
    w_source, w_once = weights([gram[k : k + 1] for k in range(6)])
    diagonal = lax.broadcasted_iota(jnp.int32, (fields, 128), 0) == lax.broadcasted_iota(
        jnp.int32, (fields, 128), 1
    )
    columns = []
    for k, w in enumerate((w_source, w_once)):
        column = jnp.sum(jnp.where(diagonal, w, 0.0), axis=1, keepdims=True)
        columns.append(column)
        weight_cols[k] = jnp.broadcast_to(column, (fields, 128))
    mixed = [parts[0, k] * columns[0] + parts[1, k] * columns[1] for k in range(4)]
    cl_send[0] = mixed[1]
    cl_send[1] = mixed[3]

    def move(src, dst, base, dx, dy):
        return pltpu.make_async_remote_copy(
            src_ref=src,
            dst_ref=dst,
            send_sem=cl_sems.at[base],
            recv_sem=cl_sems.at[base + 1],
            device_id=(i + dx, j + dy),
            device_id_type=pl.DeviceIdType.MESH,
        )

    @pl.when(j < ny - 1)
    def _():
        move(cl_send, cl_from_y, 0, 0, 1).start()

    @pl.when(j == 0)
    def _():
        cl_from_y[...] = jnp.zeros(cl_from_y.shape, jnp.float32)

    @pl.when(i == 0)
    def _():
        cl_from_x[...] = jnp.zeros(cl_from_x.shape, jnp.float32)

    @pl.when(j > 0)
    def _():
        move(cl_send, cl_from_y, 0, 0, -1).wait_recv()

    cl_forward[...] = mixed[2] + cl_from_y[1]

    @pl.when(i < nx - 1)
    def _():
        move(cl_forward, cl_from_x, 2, 1, 0).start()

    def combine(f, carry):
        ws = weight_cols[0, pl.ds(f, 1), :]
        wo = weight_cols[1, pl.ds(f, 1), :]
        answer[f] = source[f] * ws + once[f] * wo
        return carry

    lax.fori_loop(0, fields, combine, 0)

    @pl.when(i > 0)
    def _():
        move(cl_forward, cl_from_x, 2, -1, 0).wait_recv()

    own = mixed[0] + cl_from_y[0] + cl_from_x[...]
    halves = jnp.concatenate([own[:, :cl_wide], own[:, cl_wide:]], axis=0)
    high, low = split(halves)
    by = [
        dot_turned(high, waves_high[k])
        + dot_turned(low, waves_high[k])
        + dot_turned(high, waves_low[k])
        for k in range(2)
    ]
    expansion[0] = by[0][:fields] - by[1][fields:]
    expansion[1] = by[1][:fields] + by[0][fields:]

    @pl.when(j < ny - 1)
    def _():
        move(cl_send, cl_from_y, 0, 0, 1).wait_send()

    @pl.when(i < nx - 1)
    def _():
        move(cl_forward, cl_from_x, 2, 1, 0).wait_send()

    finish_sends(geo_group, 1)
    finish_sends(one_group, CHUNKS)
    finish_sends(two_group, CHUNKS)


def local(
    incident,
    positions,
    nbr_part,
    nbr_slot,
    nbr_count,
    cluster_id,
    mie,
    to_waves,
    from_waves,
    to_cluster,
    cluster_waves,
    centers,
):
    bead_count = incident.shape[2]
    field_count = incident.shape[3]
    coef_width = incident.shape[4]
    wave_count = to_waves.shape[2]
    own_pos = positions[0, 0]
    flat_index = nbr_part[0, 0] * bead_count + nbr_slot[0, 0]
    slots = jnp.arange(flat_index.shape[1], dtype=jnp.int32)
    flat_index = jnp.where(slots[None, :] < nbr_count[0, 0][:, None], flat_index, -1)
    flat_index = jnp.transpose(flat_index)
    flat_index = jnp.concatenate([flat_index, flat_index], axis=1)
    rows = jnp.arange(9 * bead_count, dtype=jnp.int32)
    times = jnp.sum((flat_index[:, None, :] == rows[None, :, None]).astype(jnp.float32), axis=0)
    times = times.reshape(9, bead_count, 2 * bead_count)
    dirs = sphere_grid(WAVE_LAT, WAVE_LON)
    bead_ids = cluster_id[0, 0]
    cluster_total = centers.shape[0]
    one_hot = (bead_ids[:, None] == jnp.arange(cluster_total, dtype=jnp.int32)[None, :]).astype(
        jnp.float32
    )
    bead_centre = jnp.sum(one_hot[:, :, None] * centers[None], axis=1)
    span_y = lax.axis_size("gy")
    code = (bead_ids // span_y - lax.axis_index("gx")) * 2 + (
        bead_ids % span_y - lax.axis_index("gy")
    )
    hot = (code[:, None] == jnp.arange(4, dtype=jnp.int32)[None, :]).astype(jnp.float32)
    pos_t = jnp.transpose(own_pos)
    column_pos = jnp.concatenate(
        [pos_t, pos_t - bead_centre, jnp.zeros((bead_count, 2), jnp.float32), hot], axis=1
    )
    column_pos = jnp.pad(column_pos, ((0, 0), (0, 116)))
    cluster_dirs = sphere_grid(CLUSTER_LAT, CLUSTER_LON)
    cl_wide = to_cluster.shape[2]
    cl_coef = cluster_waves.shape[2]
    lanes = cl_wide // 128
    flat_waves = jnp.transpose(cluster_waves, (2, 0, 1)).reshape(cl_coef, 2, lanes, 128)
    flat_waves = jnp.transpose(flat_waves, (0, 2, 1, 3)).reshape(cl_coef * 2 * lanes, 128)
    cl_rows = -(-cl_coef // 16) * 16
    row_pos = jnp.pad(jnp.concatenate([own_pos, own_pos], axis=1), ((0, 5), (0, 0)))
    nx, ny = lax.axis_size("gx"), lax.axis_size("gy")
    vmem = pl.BlockSpec(memory_space=pltpu.VMEM)
    dma = pltpu.SemaphoreType.DMA
    blocks = (field_count, 9, bead_count, coef_width)
    answer, expansion = pl.pallas_call(
        functools.partial(krylov_kernel, nx, ny),
        out_shape=(
            jax.ShapeDtypeStruct((field_count, bead_count, coef_width), jnp.float32),
            jax.ShapeDtypeStruct((2, field_count, cl_rows), jnp.float32),
        ),
        in_specs=[vmem] * 10 + [pl.BlockSpec(memory_space=pl.ANY)],
        out_specs=(vmem, vmem),
        scratch_shapes=[
            pltpu.VMEM((field_count, bead_count, coef_width), jnp.float32),
            pltpu.VMEM((coef_width, 2 * wave_count), jnp.bfloat16),
            pltpu.VMEM((coef_width, 2 * wave_count), jnp.bfloat16),
            pltpu.VMEM((8, coef_width), jnp.float32),
            pltpu.VMEM((field_count, bead_count, coef_width), jnp.float32),
            pltpu.VMEM(blocks, jnp.bfloat16),
            pltpu.VMEM(blocks, jnp.bfloat16),
            pltpu.VMEM((9, bead_count, 128), jnp.float32),
            pltpu.VMEM((9, bead_count, wave_count), jnp.float32),
            pltpu.VMEM((9, bead_count, wave_count), jnp.float32),
            pltpu.VMEM((3, 2 * bead_count, 3 * bead_count), jnp.bfloat16),
            pltpu.VMEM((9, bead_count, 2 * bead_count), jnp.float32),
            pltpu.VMEM((field_count, 2 * bead_count, 2 * wave_count), jnp.float32),
            pltpu.VMEM((coef_width, 2 * cl_wide), jnp.bfloat16),
            pltpu.VMEM((coef_width, 2 * cl_wide), jnp.bfloat16),
            pltpu.VMEM((bead_count, cl_wide), jnp.float32),
            pltpu.VMEM((bead_count, cl_wide), jnp.float32),
            pltpu.VMEM((field_count // CHUNKS, bead_count, 2 * cl_wide), jnp.float32),
            pltpu.VMEM((2, 4, field_count, 2 * cl_wide), jnp.float32),
            pltpu.VMEM((2, field_count, 128), jnp.float32),
            pltpu.VMEM((cl_rows * 2 * lanes, 128), jnp.float32),
            pltpu.VMEM((2, cl_rows, cl_wide), jnp.bfloat16),
            pltpu.VMEM((2, cl_rows, cl_wide), jnp.bfloat16),
            pltpu.VMEM((2, field_count, 2 * cl_wide), jnp.float32),
            pltpu.VMEM((2, field_count, 2 * cl_wide), jnp.float32),
            pltpu.VMEM((field_count, 2 * cl_wide), jnp.float32),
            pltpu.VMEM((field_count, 2 * cl_wide), jnp.float32),
            pltpu.VMEM((nx, 8, 128), jnp.float32),
            pltpu.VMEM((ny, 8, 128), jnp.float32),
            dma((8, 1)),
            dma((9, 1)),
            dma((8, CHUNKS)),
            dma((9, CHUNKS)),
            dma((8, CHUNKS)),
            dma((9, CHUNKS)),
            dma((nx,)),
            dma((nx,)),
            dma((ny,)),
            dma((ny,)),
            dma,
            dma((4,)),
        ],
        compiler_params=pltpu.CompilerParams(
            collective_id=0, has_side_effects=True, vmem_limit_bytes=56 * 1024 * 1024
        ),
        name="krylov",
    )(
        incident[0, 0],
        column_pos,
        row_pos,
        times,
        dirs,
        to_waves,
        jnp.transpose(from_waves, (0, 2, 1)),
        mie,
        to_cluster,
        cluster_dirs,
        flat_waves,
    )
    expansions = jnp.concatenate([expansion[0, :, :cl_coef], expansion[1, :, :cl_coef]], axis=1)
    return (jnp.transpose(answer, (1, 0, 2))[None, None], expansions[None])


def solution(mesh):
    in_specs = (
        P("gx", "gy", None, None, None),
        P("gx", "gy", None, None),
        P("gx", "gy", None, None),
        P("gx", "gy", None, None),
        P("gx", "gy", None),
        P("gx", "gy", None),
        P(),
        P(),
        P(),
        P(),
        P(),
        P(),
    )
    out_specs = (P("gx", "gy", None, None, None), P(("gx", "gy"), None, None))
    return jax.shard_map(local, mesh=mesh, in_specs=in_specs, out_specs=out_specs, check_vma=False)
```

```python
import functools
import math

import jax
import jax.numpy as jnp
import numpy as np
from jax import lax
from jax.experimental import pallas as pl
from jax.experimental.pallas import tpu as pltpu
from jax.sharding import PartitionSpec as P

WAVE_LAT = 8
WAVE_LON = 16
CLUSTER_LAT = 16
CLUSTER_LON = 32
WAVENUMBER = 3.0
EPS = 1e-06


def sphere_grid(cycle_count, cycle_size):
    polar = (np.arange(cycle_count) + 0.5) * (math.pi / cycle_count)
    stagger = 0.5 * (np.arange(cycle_count) % 2)
    azimuth = (np.arange(cycle_size)[None, :] + stagger[:, None]) * (2.0 * math.pi / cycle_size)
    height = np.cos(polar)[:, None] * np.ones_like(azimuth)
    radius = np.sin(polar)[:, None]
    grid = np.zeros((8, cycle_count * cycle_size), np.float32)
    grid[0] = (radius * np.cos(azimuth)).reshape(-1)
    grid[1] = (radius * np.sin(azimuth)).reshape(-1)
    grid[2] = height.reshape(-1)
    return grid


def weights(gram):
    ss, st, tt, su, tu, uu = [gram[k] for k in range(6)]
    beta2 = ss + EPS
    beta = jnp.sqrt(beta2)
    h11 = (ss - st) / beta2
    c = (st + EPS) / beta2
    rest = jnp.maximum((c * c * ss - 2.0 * c * st + tt) / beta2, 0.0)
    h21 = jnp.sqrt(rest + EPS)
    r = -1.0 / (beta * h21)
    p = -c * r
    h12 = (p * ss + (r - p) * st - r * su) / beta
    h22 = p * (p * ss + (r - p) * st - r * su) + r * (p * st + (r - p) * tt - r * tu)
    a = p - h12 / beta - h22 * p
    b = r - p - h22 * r
    g = -r
    q = a * a * ss + b * b * tt + g * g * uu + 2.0 * (a * b * st + a * g * su + b * g * tu)
    q = jnp.maximum(q, 0.0) + EPS
    gram_first = h11 * h11 + h21 * h21
    gram_cross = h11 * h12 + h21 * h22
    gram_second = h12 * h12 + h22 * h22 + q
    minor = h11 * h22 - h21 * h12
    det = minor * minor + q * gram_first
    y1 = beta * (gram_second * h11 - gram_cross * h12) / det
    y2 = beta * (gram_first * h12 - gram_cross * h11) / det
    return y1 / beta + y2 * p, y2 * r


CHUNKS = 4
SHIFTS = [(dx, dy) for dx in (-1, 0, 1) for dy in (-1, 0, 1)]


def krylov_kernel(
    nx,
    ny,
    incident,
    column_pos,
    row_pos,
    times,
    dirs,
    to_waves,
    from_waves,
    mie,
    to_cluster,
    cluster_dirs,
    cluster_waves,
    answer,
    expansion,
    source,
    forward_matrix,
    back_matrix,
    mie_rows,
    once,
    buf_one,
    buf_two,
    geo,
    turn_cos,
    turn_sin,
    weight,
    weight_rows,
    total,
    tc_high,
    tc_low,
    cl_cos,
    cl_sin,
    cl_samples,
    parts,
    weight_cols,
    waves,
    waves_high,
    waves_low,
    cl_send,
    cl_from_y,
    cl_forward,
    cl_from_x,
    gram_x,
    gram_y,
    geo_send,
    geo_recv,
    one_send,
    one_recv,
    two_send,
    two_recv,
    x_send,
    x_recv,
    y_send,
    y_recv,
    waves_sem,
    cl_sems,
):
    i, j = lax.axis_index("gx"), lax.axis_index("gy")
    fields, beads, width = source.shape
    wide = turn_cos.shape[2]
    step = fields // CHUNKS
    wave_rows = cluster_waves.shape[0]
    waves_copy = pltpu.make_async_copy(cluster_waves, waves.at[pl.ds(0, wave_rows)], waves_sem)
    waves_copy.start()

    def loop(first, last, body, carry, size=4):
        def several(k, carry):
            for u in range(size):
                carry = body(first + k * size + u, carry)
            return carry

        return lax.fori_loop(0, (last - first) // size, several, carry)

    def split(value):
        high = value.astype(jnp.bfloat16)
        return high, (value - high.astype(jnp.float32)).astype(jnp.bfloat16)

    def dot(a, b):
        return jnp.dot(a, b, preferred_element_type=jnp.float32)

    def dot_turned(a, b):
        return lax.dot_general(
            a, b, (((1,), (1,)), ((), ())), preferred_element_type=jnp.float32
        )

    def present(dx, dy):
        return (i + dx >= 0) & (i + dx < nx) & (j + dy >= 0) & (j + dy < ny)

    def piece(buf, p, c):
        if len(buf.shape) == 3:
            return buf.at[p]
        return buf.at[pl.ds(c * step, step), p]

    def make(buf, send, recv, slot, src, dst, c, dx, dy):
        return pltpu.make_async_remote_copy(
            src_ref=piece(buf, src, c),
            dst_ref=piece(buf, dst, c),
            send_sem=send.at[slot, c],
            recv_sem=recv.at[dst, c],
            device_id=(i + dx, j + dy),
            device_id_type=pl.DeviceIdType.MESH,
        )

    own_routes = [(0, 4, 3, 0, 1), (1, 4, 5, 0, -1), (2, 4, 1, 1, 0), (3, 4, 7, -1, 0)]
    low_routes = [(4, 3, 0, 1, 0), (5, 3, 6, -1, 0)]
    high_routes = [(6, 5, 2, 1, 0), (7, 5, 8, -1, 0)]

    def guarded(route):
        ok = present(route[3], route[4])
        if route[1] == 3:
            ok = ok & (j > 0)
        if route[1] == 5:
            ok = ok & (j < ny - 1)
        return pl.when(ok)

    def start(group, routes, c):
        for route in routes:

            @guarded(route)
            def _(route=route):
                slot, src, dst, dx, dy = route
                make(*group, slot, src, dst, c, dx, dy).start()

    def finish_sends(group, count):
        for c in range(count):
            for route in own_routes + low_routes + high_routes:

                @guarded(route)
                def _(route=route, c=c):
                    slot, src, dst, dx, dy = route
                    make(*group, slot, src, dst, c, dx, dy).wait_send()

    def arrive(group, p, c):
        dx, dy = SHIFTS[p]
        via = (dx, 0) if dx != 0 else (0, dy)

        @pl.when(present(dx, dy))
        def _():
            make(*group, 0, 4, p, c, via[0], via[1]).wait_recv()

    def forward(group, c):
        arrive(group, 3, c)
        start(group, low_routes, c)
        arrive(group, 5, c)
        start(group, high_routes, c)

    geo_group = (geo, geo_send, geo_recv)
    one_group = (buf_one, one_send, one_recv)
    two_group = (buf_two, two_send, two_recv)

    barrier = pltpu.get_barrier_semaphore()
    for d in range(1, nx):
        pl.semaphore_signal(
            barrier,
            inc=1,
            device_id=(lax.rem(i + d, nx), j),
            device_id_type=pl.DeviceIdType.MESH,
        )
    for d in range(1, ny):
        pl.semaphore_signal(
            barrier,
            inc=1,
            device_id=(i, lax.rem(j + d, ny)),
            device_id_type=pl.DeviceIdType.MESH,
        )
    geo[4] = column_pos[...]

    half = width // 2
    mie_rows[0:1, 0:half] = mie[0:1, :]
    mie_rows[0:1, half:width] = mie[0:1, :]
    mie_rows[1:2, 0:half] = -mie[1:2, :]
    mie_rows[1:2, half:width] = mie[1:2, :]
    for f in range(fields):
        value = incident[:, f, :]
        value = value * mie_rows[0:1, :] + pltpu.roll(value, half, 1) * mie_rows[1:2, :]
        source[f] = value
        buf_one[f, 4] = value.astype(jnp.bfloat16)
    forward_matrix[0:half, 0:wide] = to_waves[0]
    forward_matrix[0:half, wide : 2 * wide] = to_waves[1]
    forward_matrix[half:width, 0:wide] = -to_waves[1]
    forward_matrix[half:width, wide : 2 * wide] = to_waves[0]
    back_matrix[0:half, 0:wide] = from_waves[0]
    back_matrix[0:half, wide : 2 * wide] = -from_waves[1]
    back_matrix[half:width, 0:wide] = from_waves[1]
    back_matrix[half:width, wide : 2 * wide] = from_waves[0]
    waves[pl.ds(wave_rows, waves.shape[0] - wave_rows)] = jnp.zeros(
        (waves.shape[0] - wave_rows, 128), jnp.float32
    )
    for p, (dx, dy) in enumerate(SHIFTS):

        @pl.when(jnp.logical_not(present(dx, dy)))
        def _(p=p):
            geo[p] = jnp.zeros(geo.shape[1:], geo.dtype)

            def clear(f, carry):
                buf_one[f, p] = jnp.zeros((beads, width), jnp.bfloat16)
                buf_two[f, p] = jnp.zeros((beads, width), jnp.bfloat16)
                return carry

            lax.fori_loop(0, fields, clear, 0)

    pl.semaphore_wait(barrier, nx + ny - 2)

    start(geo_group, own_routes, 0)
    for c in range(CHUNKS):
        start(one_group, own_routes, c)
    forward(geo_group, 0)

    def geometry(p):
        pos = geo[p]
        along = (
            pos[:, 0:1] * dirs[0:1, :] + pos[:, 1:2] * dirs[1:2, :] + pos[:, 2:3] * dirs[2:3, :]
        )
        angle = WAVENUMBER * along
        turn_cos[p] = jnp.cos(angle)
        turn_sin[p] = jnp.sin(angle)
        ex = row_pos[0:1, :] - pos[:, 0:1]
        ey = row_pos[1:2, :] - pos[:, 1:2]
        ez = row_pos[2:3, :] - pos[:, 2:3]
        dist = jnp.sqrt(ex * ex + ey * ey + ez * ez)
        full = times[p] / (1.0 + dist)
        high = full.astype(jnp.bfloat16).astype(jnp.float32)
        lane = lax.broadcasted_iota(jnp.int32, full.shape, 1)
        weight_rows[p] = jnp.where(lane < beads, high, full - high)

    def turn_weights(g):
        rows = weight_rows[3 * g : 3 * g + 3].reshape(3 * beads, 2 * beads)
        weight[g] = jnp.transpose(rows).astype(jnp.bfloat16)

    cl_wide = cl_cos.shape[1]

    def cluster_setup():
        along = (
            column_pos[:, 3:4] * cluster_dirs[0:1, :]
            + column_pos[:, 4:5] * cluster_dirs[1:2, :]
            + column_pos[:, 5:6] * cluster_dirs[2:3, :]
        )
        angle = WAVENUMBER * along
        cl_cos[...] = jnp.cos(angle)
        cl_sin[...] = jnp.sin(angle)
        real_high, real_low = split(to_cluster[0])
        imag_high, imag_low = split(to_cluster[1])
        for ref, real, imag in ((tc_high, real_high, imag_high), (tc_low, real_low, imag_low)):
            ref[0:half, 0:cl_wide] = real
            ref[0:half, cl_wide : 2 * cl_wide] = imag
            ref[half:width, 0:cl_wide] = -imag
            ref[half:width, cl_wide : 2 * cl_wide] = real

    def cluster_parts(values, kind, c):
        high, low = split(values[pl.ds(c * step, step)].reshape(step * beads, width))
        smp = dot(high, tc_high[...]) + dot(low, tc_high[...]) + dot(high, tc_low[...])
        cl_samples[...] = smp.reshape(step, beads, 2 * cl_wide)

        def body(f, carry):
            re, im = cl_samples[f, :, :cl_wide], cl_samples[f, :, cl_wide:]
            co, si = cl_cos[...], cl_sin[...]
            real = re * co - im * si
            imag = re * si + im * co
            for k in range(4):
                hot = column_pos[:, 8 + k : 9 + k]
                spot = pl.ds(c * step + f, 1)
                parts[kind, k, spot, 0:cl_wide] = jnp.sum(real * hot, axis=0, keepdims=True)
                parts[kind, k, spot, cl_wide : 2 * cl_wide] = jnp.sum(
                    imag * hot, axis=0, keepdims=True
                )
            return carry

        lax.fori_loop(0, step, body, 0)

    geometry(4)
    for p in (3, 5):
        geometry(p)
    turn_weights(1)
    cluster_setup()
    for c in range(CHUNKS):
        forward(one_group, c)
        cluster_parts(source, 0, c)
    for p in (0, 1, 2, 6, 7, 8):
        arrive(geo_group, p, 0)
        geometry(p)
    turn_weights(0)
    turn_weights(2)

    def gathered(buf, f, first, count):
        rows = count * beads
        spot = pl.ds(first, count)
        low = buf[f, spot].reshape(rows, width)
        smp = jnp.dot(low, forward_matrix[...], preferred_element_type=jnp.float32)
        re, im = smp[:, :wide], smp[:, wide:]
        co = turn_cos[spot].reshape(rows, wide)
        si = turn_sin[spot].reshape(rows, wide)
        turned = jnp.concatenate(
            [
                (re * co + im * si).astype(jnp.bfloat16),
                (im * co - re * si).astype(jnp.bfloat16),
            ],
            axis=1,
        )
        return dot(weight[first // 3], turned)

    def back_turn(acc):
        inc = acc[:beads] + acc[beads:]
        re, im = inc[:, :wide], inc[:, wide:]
        co, si = turn_cos[4], turn_sin[4]
        inc = jnp.concatenate([re * co - im * si, re * si + im * co], axis=1)
        high = inc.astype(jnp.bfloat16)
        low = (inc - high.astype(jnp.float32)).astype(jnp.bfloat16)
        back = dot_turned(jnp.concatenate([high, low], axis=0), back_matrix[...])
        back = back[:beads] + back[beads:]
        return back * mie_rows[0:1, :] + pltpu.roll(back, width // 2, 1) * mie_rows[1:2, :]

    def middle(buf):
        def body(f, carry):
            total[f] = gathered(buf, f, 3, 3)
            return carry

        loop(0, fields, body, 0)

    def sides(buf, f):
        return back_turn(total[f] + gathered(buf, f, 0, 3) + gathered(buf, f, 6, 3))

    middle(buf_one)
    for c in range(CHUNKS):
        for p in (0, 1, 2, 6, 7, 8):
            arrive(one_group, p, c)

        def first(f, carry):
            value = sides(buf_one, f)
            once[f] = value
            buf_two[f, 4] = value.astype(jnp.bfloat16)
            return carry

        loop(c * step, (c + 1) * step, first, 0)
        start(two_group, own_routes, c)

    for c in range(CHUNKS):
        cluster_parts(once, 1, c)
        forward(two_group, c)
    middle(buf_two)
    waves_copy.wait()

    lanes = cl_wide // 128

    def halve(part):
        for block in range(lanes):
            rows = waves_high.shape[1]
            high, low = split(waves[pl.ds(2 * block + part, rows, stride=2 * lanes), :])
            waves_high[part, :, 128 * block : 128 * block + 128] = high
            waves_low[part, :, 128 * block : 128 * block + 128] = low

    row = lax.broadcasted_iota(jnp.int32, (8, 128), 0)
    lane = lax.broadcasted_iota(jnp.int32, (8, 128), 1)
    gram = jnp.zeros((8, 128), jnp.float32)
    for c in range(CHUNKS):
        for p in (0, 1, 2, 6, 7, 8):
            arrive(two_group, p, c)

        def second(f, gram):
            u = sides(buf_two, f)
            s, t = source[f], once[f]
            for k, (x, y) in enumerate(((s, s), (s, t), (t, t), (s, u), (t, u), (u, u))):
                value = jnp.sum(jnp.sum(x * y, axis=0, keepdims=True), axis=1, keepdims=True)
                gram = gram + jnp.where((row == k) & (lane == f), value, 0.0)
            return gram

        gram = loop(c * step, (c + 1) * step, second, gram, 2)

    def reduce_over(gram, slots, send, recv, count, peer, part):
        slots[0] = gram
        copies = []
        for d in range(1, count):
            copy = pltpu.make_async_remote_copy(
                src_ref=slots.at[0],
                dst_ref=slots.at[d],
                send_sem=send.at[d],
                recv_sem=recv.at[d],
                device_id=peer(d),
                device_id_type=pl.DeviceIdType.MESH,
            )
            copy.start()
            copies.append(copy)
        halve(part)
        for d, copy in enumerate(copies):
            copy.wait_recv()
            gram = gram + slots[d + 1]
        for copy in copies:
            copy.wait_send()
        return gram

    gram = reduce_over(gram, gram_x, x_send, x_recv, nx, lambda d: (lax.rem(i + d, nx), j), 0)
    gram = reduce_over(gram, gram_y, y_send, y_recv, ny, lambda d: (i, lax.rem(j + d, ny)), 1)
    w_source, w_once = weights([gram[k : k + 1] for k in range(6)])
    diagonal = lax.broadcasted_iota(jnp.int32, (fields, 128), 0) == lax.broadcasted_iota(
        jnp.int32, (fields, 128), 1
    )
    columns = []
    for k, w in enumerate((w_source, w_once)):
        column = jnp.sum(jnp.where(diagonal, w, 0.0), axis=1, keepdims=True)
        columns.append(column)
        weight_cols[k] = jnp.broadcast_to(column, (fields, 128))
    mixed = [parts[0, k] * columns[0] + parts[1, k] * columns[1] for k in range(4)]
    cl_send[0] = mixed[1]
    cl_send[1] = mixed[3]

    def move(src, dst, base, dx, dy):
        return pltpu.make_async_remote_copy(
            src_ref=src,
            dst_ref=dst,
            send_sem=cl_sems.at[base],
            recv_sem=cl_sems.at[base + 1],
            device_id=(i + dx, j + dy),
            device_id_type=pl.DeviceIdType.MESH,
        )

    @pl.when(j < ny - 1)
    def _():
        move(cl_send, cl_from_y, 0, 0, 1).start()

    @pl.when(j == 0)
    def _():
        cl_from_y[...] = jnp.zeros(cl_from_y.shape, jnp.float32)

    @pl.when(i == 0)
    def _():
        cl_from_x[...] = jnp.zeros(cl_from_x.shape, jnp.float32)

    @pl.when(j > 0)
    def _():
        move(cl_send, cl_from_y, 0, 0, -1).wait_recv()

    cl_forward[...] = mixed[2] + cl_from_y[1]

    @pl.when(i < nx - 1)
    def _():
        move(cl_forward, cl_from_x, 2, 1, 0).start()

    def combine(f, carry):
        ws = weight_cols[0, pl.ds(f, 1), :]
        wo = weight_cols[1, pl.ds(f, 1), :]
        answer[f] = source[f] * ws + once[f] * wo
        return carry

    lax.fori_loop(0, fields, combine, 0)

    @pl.when(i > 0)
    def _():
        move(cl_forward, cl_from_x, 2, -1, 0).wait_recv()

    own = mixed[0] + cl_from_y[0] + cl_from_x[...]
    halves = jnp.concatenate([own[:, :cl_wide], own[:, cl_wide:]], axis=0)
    high, low = split(halves)
    by = [
        dot_turned(high, waves_high[k])
        + dot_turned(low, waves_high[k])
        + dot_turned(high, waves_low[k])
        for k in range(2)
    ]
    expansion[0] = by[0][:fields] - by[1][fields:]
    expansion[1] = by[1][:fields] + by[0][fields:]

    @pl.when(j < ny - 1)
    def _():
        move(cl_send, cl_from_y, 0, 0, 1).wait_send()

    @pl.when(i < nx - 1)
    def _():
        move(cl_forward, cl_from_x, 2, 1, 0).wait_send()

    finish_sends(geo_group, 1)
    finish_sends(one_group, CHUNKS)
    finish_sends(two_group, CHUNKS)


def local(
    incident,
    positions,
    nbr_part,
    nbr_slot,
    nbr_count,
    cluster_id,
    mie,
    to_waves,
    from_waves,
    to_cluster,
    cluster_waves,
    centers,
):
    bead_count = incident.shape[2]
    field_count = incident.shape[3]
    coef_width = incident.shape[4]
    wave_count = to_waves.shape[2]
    own_pos = positions[0, 0]
    flat_index = nbr_part[0, 0] * bead_count + nbr_slot[0, 0]
    slots = jnp.arange(flat_index.shape[1], dtype=jnp.int32)
    flat_index = jnp.where(slots[None, :] < nbr_count[0, 0][:, None], flat_index, -1)
    flat_index = jnp.transpose(flat_index)
    flat_index = jnp.concatenate([flat_index, flat_index], axis=1)
    rows = jnp.arange(9 * bead_count, dtype=jnp.int32)
    times = jnp.sum((flat_index[:, None, :] == rows[None, :, None]).astype(jnp.float32), axis=0)
    times = times.reshape(9, bead_count, 2 * bead_count)
    dirs = sphere_grid(WAVE_LAT, WAVE_LON)
    bead_ids = cluster_id[0, 0]
    cluster_total = centers.shape[0]
    one_hot = (bead_ids[:, None] == jnp.arange(cluster_total, dtype=jnp.int32)[None, :]).astype(
        jnp.float32
    )
    bead_centre = jnp.sum(one_hot[:, :, None] * centers[None], axis=1)
    span_y = lax.axis_size("gy")
    code = (bead_ids // span_y - lax.axis_index("gx")) * 2 + (
        bead_ids % span_y - lax.axis_index("gy")
    )
    hot = (code[:, None] == jnp.arange(4, dtype=jnp.int32)[None, :]).astype(jnp.float32)
    pos_t = jnp.transpose(own_pos)
    column_pos = jnp.concatenate(
        [pos_t, pos_t - bead_centre, jnp.zeros((bead_count, 2), jnp.float32), hot], axis=1
    )
    column_pos = jnp.pad(column_pos, ((0, 0), (0, 116)))
    cluster_dirs = sphere_grid(CLUSTER_LAT, CLUSTER_LON)
    cl_wide = to_cluster.shape[2]
    cl_coef = cluster_waves.shape[2]
    lanes = cl_wide // 128
    flat_waves = jnp.transpose(cluster_waves, (2, 0, 1)).reshape(cl_coef, 2, lanes, 128)
    flat_waves = jnp.transpose(flat_waves, (0, 2, 1, 3)).reshape(cl_coef * 2 * lanes, 128)
    cl_rows = -(-cl_coef // 16) * 16
    row_pos = jnp.pad(jnp.concatenate([own_pos, own_pos], axis=1), ((0, 5), (0, 0)))
    nx, ny = lax.axis_size("gx"), lax.axis_size("gy")
    vmem = pl.BlockSpec(memory_space=pltpu.VMEM)
    dma = pltpu.SemaphoreType.DMA
    blocks = (field_count, 9, bead_count, coef_width)
    answer, expansion = pl.pallas_call(
        functools.partial(krylov_kernel, nx, ny),
        out_shape=(
            jax.ShapeDtypeStruct((field_count, bead_count, coef_width), jnp.float32),
            jax.ShapeDtypeStruct((2, field_count, cl_rows), jnp.float32),
        ),
        in_specs=[vmem] * 10 + [pl.BlockSpec(memory_space=pl.ANY)],
        out_specs=(vmem, vmem),
        scratch_shapes=[
            pltpu.VMEM((field_count, bead_count, coef_width), jnp.float32),
            pltpu.VMEM((coef_width, 2 * wave_count), jnp.bfloat16),
            pltpu.VMEM((coef_width, 2 * wave_count), jnp.bfloat16),
            pltpu.VMEM((8, coef_width), jnp.float32),
            pltpu.VMEM((field_count, bead_count, coef_width), jnp.float32),
            pltpu.VMEM(blocks, jnp.bfloat16),
            pltpu.VMEM(blocks, jnp.bfloat16),
            pltpu.VMEM((9, bead_count, 128), jnp.float32),
            pltpu.VMEM((9, bead_count, wave_count), jnp.float32),
            pltpu.VMEM((9, bead_count, wave_count), jnp.float32),
            pltpu.VMEM((3, 2 * bead_count, 3 * bead_count), jnp.bfloat16),
            pltpu.VMEM((9, bead_count, 2 * bead_count), jnp.float32),
            pltpu.VMEM((field_count, 2 * bead_count, 2 * wave_count), jnp.float32),
            pltpu.VMEM((coef_width, 2 * cl_wide), jnp.bfloat16),
            pltpu.VMEM((coef_width, 2 * cl_wide), jnp.bfloat16),
            pltpu.VMEM((bead_count, cl_wide), jnp.float32),
            pltpu.VMEM((bead_count, cl_wide), jnp.float32),
            pltpu.VMEM((field_count // CHUNKS, bead_count, 2 * cl_wide), jnp.float32),
            pltpu.VMEM((2, 4, field_count, 2 * cl_wide), jnp.float32),
            pltpu.VMEM((2, field_count, 128), jnp.float32),
            pltpu.VMEM((cl_rows * 2 * lanes, 128), jnp.float32),
            pltpu.VMEM((2, cl_rows, cl_wide), jnp.bfloat16),
            pltpu.VMEM((2, cl_rows, cl_wide), jnp.bfloat16),
            pltpu.VMEM((2, field_count, 2 * cl_wide), jnp.float32),
            pltpu.VMEM((2, field_count, 2 * cl_wide), jnp.float32),
            pltpu.VMEM((field_count, 2 * cl_wide), jnp.float32),
            pltpu.VMEM((field_count, 2 * cl_wide), jnp.float32),
            pltpu.VMEM((nx, 8, 128), jnp.float32),
            pltpu.VMEM((ny, 8, 128), jnp.float32),
            dma((8, 1)),
            dma((9, 1)),
            dma((8, CHUNKS)),
            dma((9, CHUNKS)),
            dma((8, CHUNKS)),
            dma((9, CHUNKS)),
            dma((nx,)),
            dma((nx,)),
            dma((ny,)),
            dma((ny,)),
            dma,
            dma((4,)),
        ],
        compiler_params=pltpu.CompilerParams(
            collective_id=0, has_side_effects=True, vmem_limit_bytes=56 * 1024 * 1024
        ),
        name="krylov",
    )(
        incident[0, 0],
        column_pos,
        row_pos,
        times,
        dirs,
        to_waves,
        jnp.transpose(from_waves, (0, 2, 1)),
        mie,
        to_cluster,
        cluster_dirs,
        flat_waves,
    )
    expansions = jnp.concatenate([expansion[0, :, :cl_coef], expansion[1, :, :cl_coef]], axis=1)
    return (jnp.transpose(answer, (1, 0, 2))[None, None], expansions[None])


def solution(mesh):
    in_specs = (
        P("gx", "gy", None, None, None),
        P("gx", "gy", None, None),
        P("gx", "gy", None, None),
        P("gx", "gy", None, None),
        P("gx", "gy", None),
        P("gx", "gy", None),
        P(),
        P(),
        P(),
        P(),
        P(),
        P(),
    )
    out_specs = (P("gx", "gy", None, None, None), P(("gx", "gy"), None, None))
    return jax.shard_map(local, mesh=mesh, in_specs=in_specs, out_specs=out_specs, check_vma=False)
```
